512 devices in a mesh: tensor: 8 (over x, core), replica: 64 (over z, y).
Axes of the slice: x: 4, y: 8, z: 8, core: 2. Of those that a mesh axis runs over, the one named last changes fastest.
Arguments:
- attention_result: bfloat16 [4096, 4096], P('replica', 'tensor'), may hold values from -6 to 6
- output_projection_weight: bfloat16 [4096, 4096], P('tensor'), may hold values from -0.09375 to 0.09375
- adapter_down_weight: bfloat16 [128, 64, 4096], P('replica', None, 'tensor'), may hold values from -0.09375 to 0.09375
- adapter_up_weight: bfloat16 [128, 64, 4096], P('replica', 'tensor'), may hold values from -0.75 to 0.75
- requested_adapters: int32 [64, 64], replicated, may hold values from 0 to 127, as said below
- slot: int32 [4096, 1], P('replica'), may hold values from 0 to 63; in each aligned block of 64 rows (0 to 63, 64 to 127, ...) at most 2 rows name the same one
Outputs:
- mixed: bfloat16 [4096, 4096], P('replica', 'tensor')
The draws below stay inside these ranges and needn't reach their ends.
Inputs may be any that keep to these rules, and one draw needn't show every extreme that they name: `requested_adapters`: each row names 64 adapters whose owners a // 2 are all different. `slot`: within the 64 sequences of one group (the rows of one device) no entry is named by more than 2 sequences, and one entry by exactly 2 in some group.
All inputs are finite; a program needn't handle non-finite values.
Results may differ from the reference program's by a relative error of at most 0.0046.
Values may be sent and summed in bfloat16 or wider, within the bound.
No kernel may reach another device: no remote copies, remote signals or barrier semaphores. Data moves between devices by JAX's collectives and lax.ppermute only.
A program may use at most 64 MiB of HBM per device.

```python
import math
import jax
import jax.numpy as jnp
import numpy as np
from jax import lax

MODEL_WIDTH = 4096
ADAPTER_RANK = 64
ADP_DEV = 2
GROUP_SEQUENCES = 64
ATTENTION_WIDTH = 4096
ADAPTER_POOL = 128
FETCH = 64
MOST = 2
SEQS = 4096
N_REPLICA = 64


def draw_requested_adapters(key, part):
    key = jax.random.fold_in(key, 7)
    row_keys = jax.random.split(key, FETCH)
    owners_rows = jax.vmap(lambda subkey: jax.random.permutation(subkey, FETCH))(row_keys)
    local_pick = jax.random.randint(jax.random.fold_in(key, 11), (FETCH, FETCH), 0, ADP_DEV)
    return (owners_rows * ADP_DEV + local_pick).astype(jnp.int32)


def level_of(own_key, extent, cuts, low, largest):
    gain, own = 1.0, jax.random.fold_in(own_key, 6)
    for position, shards_of in cuts:
        heights = jnp.exp(jax.random.uniform(jax.random.fold_in(own, position), (shards_of,), jnp.float32, low / len(cuts), largest / len(cuts)))
        gain = gain * jnp.repeat(heights, extent[position] // shards_of).reshape([-1 if axis == position else 1 for axis in range(len(extent))])
    return gain


def shared_out(own_key, own, number, rows, count, top, most, slope):
    order = jax.random.permutation(own_key, count)
    crowded, usual = portions_of(count, rows * top, most, slope, True), portions_of(count, rows * top, most, slope, False)
    places = jnp.arange(count)

    def named(tallies, offset_by):
        used = int((tallies > 0).sum())
        fixed = max(1, used // 4)
        shifted = fixed + (places - fixed + offset_by * (used - fixed)) % max(1, count - fixed)
        return jnp.zeros((count,), jnp.int32).at[order[jnp.where(places < fixed, places, shifted)]].set(jnp.asarray(tallies, jnp.int32))

    tallies = jnp.where(number % 4 == 0, named(crowded, number // 4), named(usual, number - number // 4 - 1))
    mixed = jax.random.permutation(jax.random.fold_in(own, 3), count)
    donor, receiver = mixed[0:count // 2 * 2:2], mixed[1:count // 2 * 2:2]
    margin = jnp.minimum(tallies[donor] - 1, most - tallies[receiver]) // 2
    margin = jnp.where((donor == order[0]) | (receiver == order[0]) | (tallies[receiver] == 0), 0, jnp.maximum(margin, 0))
    shifted = jax.random.randint(jax.random.fold_in(own, 4), (count // 2,), 0, 1 << 20) % (margin + 1)
    tallies = tallies.at[donor].add(-shifted).at[receiver].add(shifted)
    members = jnp.searchsorted(jnp.cumsum(tallies), jnp.arange(rows * top), side="right").astype(jnp.int32)
    table = members.reshape(top, rows).T
    table = table[jax.random.permutation(jax.random.fold_in(own, 1), rows)]
    offset_by = jax.random.randint(jax.random.fold_in(own, 2), (rows, 1), 0, top)
    return jnp.take_along_axis(table, (jnp.arange(top)[None, :] + offset_by) % top, axis=1)


def portions_of(amount, total, reach, skew, full):
    portions = [(1 << 20) // math.isqrt(rank ** skew) + 1 for rank in range(1, amount + 1)]
    largest = reach if full else min(reach, max(-(-total // amount), total * portions[0] // sum(portions)))
    least = 1 if total - largest >= amount - 1 else 0
    given, surplus = [largest] + [least] * (amount - 1), total - largest - least * (amount - 1)
    while surplus > 0:
        free = [i for i in range(1, amount) if given[i] < largest] or [i for i in range(1, amount) if given[i] < reach]
        mass, budget = sum([portions[i] for i in free]), surplus
        for i in free:
            addition = min(reach - given[i], max(1, budget * portions[i] // mass), surplus)
            given[i] = given[i] + addition
            surplus = surplus - addition
    return np.array(given)


def gaussian(key, dims, spread, bound, cuts=(), kind=jnp.bfloat16):
    array = spread * jax.random.normal(key, dims, jnp.float32)
    if cuts:
        array = array * level_of(key, dims, cuts, -0.22, 0.18)
    return jnp.clip(array, -bound, bound).astype(kind)


def setup_inputs(seed: int = 0) -> dict:
    key_of = jax.random.split(jax.random.key(seed), 7)
    attention_result = gaussian(key_of[0], (SEQS, ATTENTION_WIDTH), 1.0, 6.0, ((0, 64), (1, 8)))
    output_projection_weight = gaussian(key_of[1], (ATTENTION_WIDTH, MODEL_WIDTH), ATTENTION_WIDTH ** -0.5, 0.09375, ((0, 8),))
    adapter_down_weight = gaussian(key_of[2], (ADAPTER_POOL, ADAPTER_RANK, ATTENTION_WIDTH), ATTENTION_WIDTH ** -0.5, 0.09375, ((0, 64), (2, 8)))
    adapter_up_weight = gaussian(key_of[3], (ADAPTER_POOL, ADAPTER_RANK, MODEL_WIDTH), ADAPTER_RANK ** -0.5, 0.75, ((0, 64), (1, 8)))
    requested_adapters = draw_requested_adapters(jax.random.fold_in(key_of[6], 71), 0)
    slot_keys = jax.random.split(jax.random.fold_in(key_of[5], 1), SEQS // GROUP_SEQUENCES)
    slot_turns = jax.random.permutation(jax.random.fold_in(key_of[5], 3), SEQS // GROUP_SEQUENCES)
    slot = jax.vmap(lambda own, number: shared_out(jax.random.fold_in(key_of[5], 2), own, number, GROUP_SEQUENCES, FETCH, 1, MOST, 1))(slot_keys, slot_turns).reshape((SEQS, 1))
    return dict(attention_result=attention_result, output_projection_weight=output_projection_weight, adapter_down_weight=adapter_down_weight, adapter_up_weight=adapter_up_weight, requested_adapters=requested_adapters, slot=slot)


adapter_scale = 2.0


def reference(attention_result, output_projection_weight, adapter_down_weight, adapter_up_weight, requested_adapters, slot):
    base_contribution = jnp.dot(attention_result, output_projection_weight, preferred_element_type=jnp.float32)
    group_of = (jnp.arange(GROUP_SEQUENCES * N_REPLICA) // GROUP_SEQUENCES).astype(jnp.int32)
    adapter = requested_adapters[group_of, slot[:, 0]].astype(jnp.int32)
    input_arrays = attention_result.reshape(N_REPLICA, GROUP_SEQUENCES, attention_result.shape[1])
    selected_adapter = adapter.reshape(N_REPLICA, GROUP_SEQUENCES)

    def group_breakdown(pieces):
        replica_group_rows, replica_group_ids = pieces
        down_weight_pages = jnp.take(adapter_down_weight, replica_group_ids, axis=0).astype(jnp.float32)
        adapter_input = jnp.einsum("me,moe->mo", replica_group_rows.astype(jnp.float32), down_weight_pages)
        adapter_lowrank = (adapter_scale * adapter_input).astype(jnp.bfloat16)
        up_weight_pages = jnp.take(adapter_up_weight, replica_group_ids, axis=0).astype(jnp.float32)
        return jnp.einsum("zm,zml->zl", adapter_lowrank.astype(jnp.float32), up_weight_pages)

    adapter_output = lax.map(group_breakdown, (input_arrays, selected_adapter)).reshape(GROUP_SEQUENCES * N_REPLICA, MODEL_WIDTH)
    return (base_contribution + adapter_output).astype(jnp.bfloat16)
```

```python
import jax
import jax.numpy as jnp
from jax import lax
from jax.sharding import PartitionSpec as P

adapter_scale = 2.0
most = 2
bf16 = jnp.bfloat16
f32 = jnp.float32


def local(attention, weight, down, up, requested, slot):
    group = lax.axis_index("replica")
    rows, features = attention.shape
    present, rank, _ = down.shape
    owners = requested.shape[0]
    columns = weight.shape[1] // lax.axis_size("tensor")

    entries = jnp.take(requested, group, axis=0)
    named = (slot == jnp.arange(entries.shape[0])[None, :]).astype(bf16)
    earlier = jnp.dot(jnp.tril(jnp.ones((rows, rows), bf16), -1), named, preferred_element_type=f32)
    place = jnp.sum(earlier * named, axis=1).astype(jnp.int32)
    owner = jnp.sum(named.astype(jnp.int32) * (entries // present)[None, :], axis=1)
    goes = (owner * most + place)[:, None] == jnp.arange(owners * most)[None, :]
    goes = goes.astype(bf16)
    sent = jnp.dot(goes.T, attention, preferred_element_type=f32).astype(bf16)
    here = lax.all_to_all(sent.reshape(owners, most, features), "replica", 0, 0, tiled=True)

    base = jnp.dot(attention, weight, preferred_element_type=f32).astype(bf16)
    base = lax.psum_scatter(base, "tensor", scatter_dimension=1, tiled=True)

    mine = requested // present == group
    which = jnp.sum(jnp.where(mine, requested % present, 0), axis=1)
    which = jnp.repeat(which, most)
    chosen = which[:, None] == jnp.arange(present)[None, :]

    low = jnp.dot(
        here.reshape(owners * most, features),
        down.reshape(present * rank, features).T,
        preferred_element_type=f32,
    ).reshape(owners * most, present, rank)
    low = jnp.sum(jnp.where(chosen[:, :, None], low, 0.0), axis=1).astype(bf16)
    shards = lax.axis_size("tensor")
    low = lax.all_to_all(
        jnp.broadcast_to(low, (shards,) + low.shape), "tensor", 0, 0, tiled=True
    )
    low = (adapter_scale * jnp.sum(low.astype(f32), axis=0)).astype(bf16)

    up = up.reshape(present, up.shape[1], shards, columns).transpose(2, 0, 1, 3)
    up = lax.all_to_all(up, "tensor", 0, 0, tiled=True)
    up = up.transpose(1, 0, 2, 3).reshape(present * rank, columns)
    low = jnp.where(chosen[:, :, None], low[:, None, :], jnp.zeros((), bf16))
    out = jnp.dot(
        low.reshape(owners * most, present * rank), up, preferred_element_type=f32
    ).astype(bf16)
    back = lax.all_to_all(out.reshape(owners, most, columns), "replica", 0, 0, tiled=True)
    out = jnp.dot(goes, back.reshape(owners * most, columns), preferred_element_type=f32)
    return (base.astype(f32) + out).astype(bf16)


def solution(mesh):
    in_specs = (
        P("replica", "tensor"),
        P("tensor", None),
        P("replica", None, "tensor"),
        P("replica", "tensor", None),
        P(),
        P("replica", None),
    )
    out_specs = P("replica", "tensor")
    return jax.shard_map(local, mesh=mesh, in_specs=in_specs, out_specs=out_specs, check_vma=False)
```

```python
import functools

import jax
import jax.numpy as jnp
from jax import lax
from jax.experimental import pallas as pl
from jax.experimental.pallas import tpu as pltpu
from jax.sharding import PartitionSpec as P

adapter_scale = 2.0
most = 2
lanes = 128
block = 16
bf16 = jnp.bfloat16
f32 = jnp.float32
i32 = jnp.int32


def iota(shape, axis):
    return lax.broadcasted_iota(i32, shape, axis)


def one_hot(hit):
    return jnp.where(hit, 1.0, 0.0).astype(bf16)


def times(a, b):
    return jnp.dot(a, b, preferred_element_type=f32)


def place_rows(present, requested_ref, slot_ref):
    group = lax.axis_index("replica")
    owners = requested_ref.shape[0]
    count = slot_ref.shape[0]
    square = (count, count)
    slot = jnp.sum(
        jnp.where(iota(square, 0) == iota(square, 1), slot_ref[...], 0), axis=0, keepdims=True
    )
    mine = iota(requested_ref.shape, 0) == group
    entries = jnp.sum(jnp.where(mine, requested_ref[...], 0), axis=0, keepdims=True)
    named = iota((owners, count), 0) == slot
    before = one_hot(iota(square, 0) < iota(square, 1))
    earlier = times(one_hot(named), before)
    place = jnp.sum(jnp.where(named, earlier, 0.0), axis=0, keepdims=True)
    owner = lax.div(entries, jnp.int32(present)).astype(f32).astype(bf16)
    owner = times(jnp.broadcast_to(owner, (block, owners)), one_hot(named))[:1]
    return (owner * float(most) + place).astype(i32)


def send_kernel(present, requested_ref, slot_ref, attention_ref, sent_ref, goes_ref):
    goes = place_rows(present, requested_ref, slot_ref)
    count, features = attention_ref.shape
    chunks = features // lanes
    goes_ref[...] = jnp.sum(
        jnp.where(iota((count, count), 0) == iota((count, count), 1), goes, 0), axis=1, keepdims=True
    )
    target = jnp.concatenate([goes * chunks + k for k in range(chunks)], axis=1)
    stacked = jnp.concatenate(
        [attention_ref[:, k * lanes : (k + 1) * lanes] for k in range(chunks)], axis=0
    )
    pick = one_hot(iota((sent_ref.shape[0], chunks * count), 0) == target)
    sent_ref[...] = times(pick, stacked).astype(bf16)


def base_kernel(attention_ref, weight_ref, up_ref, out_ref):
    rows = attention_ref.shape[0]
    chunks = weight_ref.shape[1] // lanes
    base = times(attention_ref[...], weight_ref[...]).astype(bf16)
    for k in range(chunks):
        out_ref[0, k * rows : (k + 1) * rows, :] = base[:, k * lanes : (k + 1) * lanes]
    up = jnp.concatenate([up_ref[a] for a in range(up_ref.shape[0])], axis=0)
    height = up.shape[0]
    for k in range(chunks):
        out_ref[0, chunks * rows + k * height : chunks * rows + (k + 1) * height, :] = up[
            :, k * lanes : (k + 1) * lanes
        ]


def named_here(requested_ref, present):
    owner = lax.axis_index("replica")
    requested = requested_ref[...]
    mine = lax.div(requested, jnp.int32(present)) == owner
    return jnp.sum(
        jnp.where(mine, lax.rem(requested, jnp.int32(present)), 0), axis=1, keepdims=True
    )


def interleave(parts, backward):
    shape = (parts * block, parts * block)
    row, column = iota(shape, 0), iota(shape, 1)
    if backward:
        row, column = column, row
    return one_hot(lax.rem(row, jnp.int32(parts)) * block + lax.div(row, jnp.int32(parts)) == column)


def low_kernel(requested_ref, here_ref, down_ref, message_ref, out_ref, rows_ref):
    del message_ref
    present, rank, features = down_ref.shape
    groups = requested_ref.shape[0]
    chunks = features // lanes
    parts = most * chunks
    order = interleave(parts, True)
    for b in range(groups // block):
        rows = times(order, here_ref[b * parts * block : (b + 1) * parts * block, :]).astype(bf16)
        for j in range(parts):
            place, k = divmod(j, chunks)
            rows_ref[
                place * groups + b * block : place * groups + (b + 1) * block,
                k * lanes : (k + 1) * lanes,
            ] = rows[j * block : (j + 1) * block, :]
    down = jnp.concatenate([down_ref[a] for a in range(present)], axis=0)
    low = lax.dot_general(
        rows_ref[...], down, (((1,), (1,)), ((), ())), preferred_element_type=f32
    )
    which = named_here(requested_ref, present)
    places = []
    for place in range(most):
        one = low[place * groups : (place + 1) * groups, :]
        places.append(
            sum(
                jnp.where(which == a, one[:, a * rank : (a + 1) * rank], 0.0)
                for a in range(present)
            )
        )
    low = jnp.concatenate(places, axis=1).astype(bf16)
    for peer in range(out_ref.shape[0]):
        out_ref[peer] = low


def result_kernel(present, requested_ref, low_ref, up_ref, out_ref, rows_ref):
    shards, groups, width = low_ref.shape
    rank = width // most
    window = rank // shards
    depth = shards * present * window
    chunks = up_ref.shape[1] // (present * window)
    parts = most * chunks
    low = low_ref[0].astype(f32)
    for peer in range(1, shards):
        low = low + low_ref[peer].astype(f32)
    low = (adapter_scale * low).astype(bf16)
    up = jnp.concatenate(
        [
            jnp.concatenate(
                [up_ref[peer, k * present * window : (k + 1) * present * window, :] for peer in range(shards)],
                axis=0,
            )
            for k in range(chunks)
        ],
        axis=1,
    )
    which = named_here(requested_ref, present)
    source, target = iota((width, depth), 0), iota((width, depth), 1)
    shard = lax.div(target, jnp.int32(present * window))
    rank_of = shard * window + lax.rem(target, jnp.int32(window))
    adapter = iota((groups, depth), 1)
    adapter = lax.rem(lax.div(adapter, jnp.int32(window)), jnp.int32(present))
    order = interleave(parts, False)
    results = []
    for place in range(most):
        spread = times(low, one_hot(source == place * rank + rank_of)).astype(bf16)
        spread = jnp.where(adapter == which, spread, jnp.zeros_like(spread))
        results.append(times(spread, up).astype(bf16))
    for b in range(groups // block):
        for j in range(parts):
            place, k = divmod(j, chunks)
            rows_ref[j * block : (j + 1) * block, :] = results[place][
                b * block : (b + 1) * block, k * lanes : (k + 1) * lanes
            ]
        out_ref[b * parts * block : (b + 1) * parts * block, :] = times(order, rows_ref[...]).astype(bf16)


def sum_kernel(base_ref, out_ref):
    total = base_ref[0].astype(f32)
    for peer in range(1, base_ref.shape[0]):
        total = total + base_ref[peer].astype(f32)
    out_ref[...] = total


def finish_kernel(goes_ref, base_ref, back_ref, out_ref):
    rows, columns = out_ref.shape
    chunks = columns // lanes
    goes = goes_ref[...] * chunks
    for k in range(chunks):
        pick = one_hot(iota((rows, back_ref.shape[0]), 1) == goes + k)
        total = base_ref[k * rows : (k + 1) * rows, :] + times(pick, back_ref[...])
        out_ref[:, k * lanes : (k + 1) * lanes] = total.astype(bf16)


def whole(shape):
    return pl.BlockSpec(shape, lambda *_: (0,) * len(shape))


def local(attention, weight, down, up, requested, slot):
    rows, features = attention.shape
    present, rank, _ = down.shape
    window = up.shape[1]
    groups = requested.shape[0]
    shards = lax.axis_size("tensor")
    columns = weight.shape[1] // shards
    parts = most * features // lanes
    out_parts = most * columns // lanes
    call = pl.pallas_call

    sent, goes = call(
        functools.partial(send_kernel, present),
        grid=(),
        out_shape=(
            jax.ShapeDtypeStruct((groups * parts, lanes), bf16),
            jax.ShapeDtypeStruct((rows, 1), i32),
        ),
        in_specs=[whole(requested.shape), whole(slot.shape), whole(attention.shape)],
        out_specs=(whole((groups * parts, lanes)), whole((rows, 1))),
    )(requested, slot, attention)
    here = lax.all_to_all(sent.reshape(groups, parts, lanes), "replica", 0, 0, tiled=True)

    chunks = columns // lanes
    base_rows = chunks * rows
    up_rows = chunks * present * window
    low_rows = groups
    total_rows = base_rows + up_rows + low_rows
    message = call(
        base_kernel,
        grid=(shards,),
        out_shape=jax.ShapeDtypeStruct((shards, total_rows, lanes), bf16),
        in_specs=[
            whole(attention.shape),
            pl.BlockSpec((features, columns), lambda i: (0, i)),
            pl.BlockSpec((present, window, columns), lambda i: (0, 0, i)),
        ],
        out_specs=pl.BlockSpec((1, total_rows, lanes), lambda i: (i, 0, 0)),
        cost_estimate=pl.CostEstimate(
            flops=2 * rows * features * weight.shape[1],
            bytes_accessed=2 * weight.size + 2 * shards * total_rows * lanes,
            transcendentals=0,
        ),
    )(attention, weight, up)

    low_block = pl.BlockSpec(
        (shards, low_rows, lanes), lambda *_: (0, (base_rows + up_rows) // low_rows, 0)
    )
    message = call(
        low_kernel,
        grid=(1,),
        out_shape=jax.ShapeDtypeStruct(message.shape, bf16),
        in_specs=[
            whole(requested.shape),
            whole((groups * parts, lanes)),
            whole(down.shape),
            pl.BlockSpec(memory_space=pl.ANY),
        ],
        out_specs=low_block,
        scratch_shapes=[pltpu.VMEM((most * groups, features), bf16)],
        input_output_aliases={3: 0},
    )(requested, here.reshape(groups * parts, lanes), down, message)
    message = lax.all_to_all(message, "tensor", 0, 0, tiled=True)

    result = call(
        functools.partial(result_kernel, present),
        grid=(1,),
        out_shape=jax.ShapeDtypeStruct((groups * out_parts, lanes), bf16),
        in_specs=[
            whole(requested.shape),
            low_block,
            pl.BlockSpec((shards, up_rows, lanes), lambda *_: (0, base_rows // up_rows, 0)),
        ],
        out_specs=whole((groups * out_parts, lanes)),
        scratch_shapes=[pltpu.VMEM((out_parts * block, lanes), bf16)],
    )(requested, message, message)
    back = lax.all_to_all(result.reshape(groups, out_parts, lanes), "replica", 0, 0, tiled=True)

    base = call(
        sum_kernel,
        grid=(1,),
        out_shape=jax.ShapeDtypeStruct((base_rows, lanes), f32),
        in_specs=[whole((shards, base_rows, lanes))],
        out_specs=whole((base_rows, lanes)),
        cost_estimate=pl.CostEstimate(
            flops=shards * base_rows * lanes,
            bytes_accessed=2 * shards * base_rows * lanes,
            transcendentals=0,
        ),
    )(message)
    return call(
        finish_kernel,
        grid=(),
        out_shape=jax.ShapeDtypeStruct((rows, columns), bf16),
        in_specs=[
            whole((rows, 1)),
            whole((base_rows, lanes)),
            whole((groups * out_parts, lanes)),
        ],
        out_specs=whole((rows, columns)),
    )(goes, base, back.reshape(groups * out_parts, lanes))


def solution(mesh):
    in_specs = (
        P("replica", "tensor"),
        P("tensor", None),
        P("replica", None, "tensor"),
        P("replica", "tensor", None),
        P(),
        P("replica", None),
    )
    out_specs = P("replica", "tensor")
    return jax.shard_map(local, mesh=mesh, in_specs=in_specs, out_specs=out_specs, check_vma=False)
```

```python
import functools

import jax
import jax.numpy as jnp
from jax import lax
from jax.experimental import pallas as pl
from jax.experimental.pallas import tpu as pltpu
from jax.sharding import PartitionSpec as P

adapter_scale = 2.0
most = 2
lanes = 128
block = 16
ahead = 3
bf16 = jnp.bfloat16
f32 = jnp.float32
i32 = jnp.int32


def iota(shape, axis):
    return lax.broadcasted_iota(i32, shape, axis)


def one_hot(hit):
    return jnp.where(hit, 1.0, 0.0).astype(bf16)


def times(a, b):
    return jnp.dot(a, b, preferred_element_type=f32)


def column_of(row):
    size = row.shape[1]
    square = (size, size)
    return jnp.sum(jnp.where(iota(square, 0) == iota(square, 1), row, 0), axis=1, keepdims=True)


def place_rows(present, requested_ref, slot_ref):
    group = lax.axis_index("replica")
    owners = requested_ref.shape[0]
    count = slot_ref.shape[1]
    mine = iota(requested_ref.shape, 0) == group
    entries = jnp.sum(jnp.where(mine, requested_ref[...], 0), axis=0, keepdims=True)
    named = iota((owners, count), 0) == slot_ref[...]
    before = one_hot(iota((count, count), 0) < iota((count, count), 1))
    earlier = times(one_hot(named), before)
    place = jnp.sum(jnp.where(named, earlier, 0.0), axis=0, keepdims=True)
    owner = lax.div(entries, jnp.int32(present)).astype(f32).astype(bf16)
    owner = times(jnp.broadcast_to(owner, (block, owners)), one_hot(named))[:1]
    return (owner * float(most) + place).astype(i32)


def send_kernel(present, requested_ref, slot_ref, attention_ref, sent_ref, goes_ref):
    goes = place_rows(present, requested_ref, slot_ref)
    count, features = attention_ref.shape
    chunks = features // lanes
    goes_ref[...] = goes
    target = jnp.concatenate([goes * chunks + k for k in range(chunks)], axis=1)
    stacked = jnp.concatenate(
        [attention_ref[:, k * lanes : (k + 1) * lanes] for k in range(chunks)], axis=0
    )
    pick = one_hot(iota((sent_ref.shape[0], chunks * count), 0) == target)
    sent_ref[...] = times(pick, stacked).astype(bf16)


def base_kernel(
    attention_ref, weight_ref, mine_ref, other_ref, rows, weights, arrived
):
    chips, _, columns = mine_ref.shape
    index = lax.axis_index("tensor")
    core = lax.rem(index, 2)
    chip = lax.div(index, 2)

    def fetch(slot):
        away = (0, 2, 1, 3)[slot // 2]
        device = 2 * (chip ^ away) + (core if slot % 2 else 1 - core)
        start = pl.multiple_of(device * columns, columns)
        return pltpu.make_async_copy(
            weight_ref.at[:, pl.ds(start, columns)], weights.at[slot], arrived.at[slot]
        )

    load = pltpu.make_async_copy(attention_ref, rows, arrived.at[2 * chips])
    load.start()
    for slot in range(ahead):
        fetch(slot).start()
    load.wait()
    for slot in range(2 * chips):
        fetch(slot).wait()
        if slot + ahead < 2 * chips:
            fetch(slot + ahead).start()
        base = times(rows[...], weights[slot])
        if slot % 2:
            mine_ref[slot // 2] = base
        else:
            other_ref[slot // 2] = base.astype(bf16)


def chip_kernel(mine_ref, got_ref, near_ref, far_ref):
    half = near_ref.shape[0]
    near_ref[...] = mine_ref[:half] + got_ref[:half].astype(f32)
    far_ref[...] = (mine_ref[half:] + got_ref[half:].astype(f32)).astype(bf16)


def pair_kernel(goes_ref, near_ref, got_ref, mine_ref, send_ref, pick_ref):
    mine_ref[...] = near_ref[0] + got_ref[0].astype(f32)
    send_ref[...] = (near_ref[1] + got_ref[1].astype(f32)).astype(bf16)
    rows, columns = mine_ref.shape
    chunks = columns // lanes
    goes = column_of(goes_ref[...]) * chunks
    for k in range(chunks):
        pick_ref[k * rows : (k + 1) * rows, :] = one_hot(
            iota((rows, pick_ref.shape[1]), 1) == goes + k
        )


def named_here(requested_ref, present):
    owner = lax.axis_index("replica")
    requested = requested_ref[...]
    mine = lax.div(requested, jnp.int32(present)) == owner
    return jnp.sum(
        jnp.where(mine, lax.rem(requested, jnp.int32(present)), 0), axis=1, keepdims=True
    )


def interleave(parts, backward):
    shape = (parts * block, parts * block)
    row, column = iota(shape, 0), iota(shape, 1)
    if backward:
        row, column = column, row
    return one_hot(lax.rem(row, jnp.int32(parts)) * block + lax.div(row, jnp.int32(parts)) == column)


def low_kernel(requested_ref, here_ref, down_ref, up_ref, out_ref, rows_ref):
    present, rank, features = down_ref.shape
    groups = requested_ref.shape[0]
    chunks = features // lanes
    parts = most * chunks
    order = interleave(parts, True)
    for b in range(groups // block):
        rows = times(order, here_ref[b * parts * block : (b + 1) * parts * block, :]).astype(bf16)
        for j in range(parts):
            place, k = divmod(j, chunks)
            rows_ref[
                place * groups + b * block : place * groups + (b + 1) * block,
                k * lanes : (k + 1) * lanes,
            ] = rows[j * block : (j + 1) * block, :]
    down = jnp.concatenate([down_ref[a] for a in range(present)], axis=0)
    low = lax.dot_general(
        rows_ref[...], down, (((1,), (1,)), ((), ())), preferred_element_type=f32
    )
    which = named_here(requested_ref, present)
    places = []
    for place in range(most):
        one = low[place * groups : (place + 1) * groups, :]
        places.append(
            sum(
                jnp.where(which == a, one[:, a * rank : (a + 1) * rank], 0.0)
                for a in range(present)
            )
        )
    low = jnp.concatenate(places, axis=1).astype(bf16)
    up = jnp.concatenate([up_ref[a] for a in range(present)], axis=0)
    height = up.shape[0]
    shards = out_ref.shape[0]
    columns = up.shape[1] // shards
    for peer in range(shards):
        for k in range(columns // lanes):
            out_ref[peer, k * height : (k + 1) * height, :] = up[
                :, peer * columns + k * lanes : peer * columns + (k + 1) * lanes
            ]
        out_ref[peer, out_ref.shape[1] - groups :, :] = low


def result_kernel(present, requested_ref, low_ref, up_ref, out_ref, rows_ref):
    shards, groups, width = low_ref.shape
    rank = width // most
    window = rank // shards
    depth = shards * present * window
    chunks = up_ref.shape[1] // (present * window)
    parts = most * chunks
    low = low_ref[0].astype(f32)
    for peer in range(1, shards):
        low = low + low_ref[peer].astype(f32)
    low = (adapter_scale * low).astype(bf16)
    up = jnp.concatenate(
        [
            jnp.concatenate(
                [up_ref[peer, k * present * window : (k + 1) * present * window, :] for peer in range(shards)],
                axis=0,
            )
            for k in range(chunks)
        ],
        axis=1,
    )
    which = named_here(requested_ref, present)
    source, target = iota((width, depth), 0), iota((width, depth), 1)
    shard = lax.div(target, jnp.int32(present * window))
    rank_of = shard * window + lax.rem(target, jnp.int32(window))
    adapter = iota((groups, depth), 1)
    adapter = lax.rem(lax.div(adapter, jnp.int32(window)), jnp.int32(present))
    order = interleave(parts, False)
    results = []
    for place in range(most):
        spread = times(low, one_hot(source == place * rank + rank_of)).astype(bf16)
        spread = jnp.where(adapter == which, spread, jnp.zeros_like(spread))
        results.append(times(spread, up).astype(bf16))
    for b in range(groups // block):
        for j in range(parts):
            place, k = divmod(j, chunks)
            rows_ref[j * block : (j + 1) * block, :] = results[place][
                b * block : (b + 1) * block, k * lanes : (k + 1) * lanes
            ]
        out_ref[b * parts * block : (b + 1) * parts * block, :] = times(order, rows_ref[...]).astype(bf16)


def lora_kernel(pick_ref, back_ref, out_ref):
    rows, columns = out_ref.shape
    mine = times(pick_ref[...], back_ref[...])
    for k in range(columns // lanes):
        out_ref[:, k * lanes : (k + 1) * lanes] = mine[k * rows : (k + 1) * rows, :]


def finish_kernel(lora_ref, mine_ref, got_ref, out_ref):
    out_ref[...] = (mine_ref[...] + got_ref[...].astype(f32) + lora_ref[...]).astype(bf16)


def whole(shape):
    return pl.BlockSpec(shape, lambda *_: (0,) * len(shape))


def call(kernel, out_shape, in_specs, out_specs, cost=(0, 0), limit=4, **options):
    return pl.pallas_call(
        kernel,
        grid=(1,),
        out_shape=out_shape,
        in_specs=in_specs,
        out_specs=out_specs,
        compiler_params=pltpu.CompilerParams(vmem_limit_bytes=limit << 20),
        cost_estimate=pl.CostEstimate(flops=cost[0], bytes_accessed=cost[1], transcendentals=0),
        **options,
    )


def local(attention, weight, down, up, requested, slot):
    rows, features = attention.shape
    present, rank, _ = down.shape
    window = up.shape[1]
    groups = requested.shape[0]
    shards = lax.axis_size("tensor")
    columns = weight.shape[1] // shards
    parts = most * features // lanes
    out_parts = most * columns // lanes
    chunks = columns // lanes
    shape = jax.ShapeDtypeStruct

    sent, goes = call(
        functools.partial(send_kernel, present),
        (shape((groups * parts, lanes), bf16), shape((1, rows), i32)),
        [whole(requested.shape), whole((1, rows)), whole(attention.shape)],
        (whole((groups * parts, lanes)), whole((1, rows))),
        cost=(1 << 34, 1 << 20),
        limit=56,
    )(requested, slot.reshape(1, rows), attention)
    here = lax.all_to_all(sent.reshape(groups, parts, lanes), "replica", 0, 0, tiled=True)

    chips = shards // 2
    tile = (rows, columns)
    mine, other = call(
        base_kernel,
        (shape((chips,) + tile, f32), shape((chips,) + tile, bf16)),
        [pl.BlockSpec(memory_space=pl.ANY), pl.BlockSpec(memory_space=pl.ANY)],
        (whole((chips,) + tile), whole((chips,) + tile)),
        cost=(1 << 34, 1 << 20),
        limit=10,
        scratch_shapes=[
            pltpu.VMEM((rows, features), bf16),
            pltpu.VMEM((shards, features, columns), bf16),
            pltpu.SemaphoreType.DMA((shards + 1,)),
        ],
    )(attention, weight)
    got = lax.ppermute(other, "tensor", [(i, i ^ 1) for i in range(shards)])

    up_rows = chunks * present * window
    message = call(
        low_kernel,
        shape((shards, up_rows + groups, lanes), bf16),
        [whole(requested.shape), whole((groups * parts, lanes)), whole(down.shape), whole(up.shape)],
        whole((shards, up_rows + groups, lanes)),
        cost=(6 * groups * parts * lanes * lanes, 6 * groups * parts * lanes),
        scratch_shapes=[pltpu.VMEM((most * groups, features), bf16)],
    )(requested, here.reshape(groups * parts, lanes), down, up)
    message = lax.all_to_all(message, "tensor", 0, 0, tiled=True)

    near, far = call(
        chip_kernel,
        (shape((chips // 2,) + tile, f32), shape((chips // 2,) + tile, bf16)),
        [whole((chips,) + tile), whole((chips,) + tile)],
        (whole((chips // 2,) + tile), whole((chips // 2,) + tile)),
        cost=(1 << 34, 1 << 20),
    )(mine, got)
    got = lax.ppermute(far, "tensor", [(i, i ^ 2) for i in range(shards)])

    result = call(
        functools.partial(result_kernel, present),
        shape((groups * out_parts, lanes), bf16),
        [
            whole(requested.shape),
            pl.BlockSpec((shards, groups, lanes), lambda *_: (0, up_rows // groups, 0)),
            pl.BlockSpec((shards, up_rows, lanes), lambda *_: (0, 0, 0)),
        ],
        whole((groups * out_parts, lanes)),
        cost=(6 * groups * parts * lanes * lanes, 6 * groups * parts * lanes),
        scratch_shapes=[pltpu.VMEM((out_parts * block, lanes), bf16)],
    )(requested, message, message)
    back = lax.all_to_all(result.reshape(groups, out_parts, lanes), "replica", 0, 0, tiled=True)

    mine, send, pick = call(
        pair_kernel,
        (shape(tile, f32), shape(tile, bf16), shape((chunks * rows, groups * out_parts), bf16)),
        [whole((1, rows)), whole((chips // 2,) + tile), whole((chips // 2,) + tile)],
        (whole(tile), whole(tile), whole((chunks * rows, groups * out_parts))),
        cost=(1 << 34, 1 << 20),
    )(goes, near, got)
    got = lax.ppermute(send, "tensor", [(i, i ^ 4) for i in range(shards)])

    lora = call(
        lora_kernel,
        shape(tile, f32),
        [whole((chunks * rows, groups * out_parts)), whole((groups * out_parts, lanes))],
        whole(tile),
        cost=(2 * chunks * rows * groups * out_parts * lanes, 4 * chunks * rows * groups * out_parts),
    )(pick, back.reshape(groups * out_parts, lanes))
    return call(
        finish_kernel,
        shape(tile, bf16),
        [whole(tile), whole(tile), whole(tile)],
        whole(tile),
    )(lora, mine, got)


def solution(mesh):
    in_specs = (
        P("replica", "tensor"),
        P("tensor", None),
        P("replica", None, "tensor"),
        P("replica", "tensor", None),
        P(),
        P("replica", None),
    )
    out_specs = P("replica", "tensor")
    return jax.shard_map(local, mesh=mesh, in_specs=in_specs, out_specs=out_specs, check_vma=False)
```

```python
import functools

import jax
import jax.numpy as jnp
from jax import lax
from jax.experimental import pallas as pl
from jax.experimental.pallas import tpu as pltpu
from jax.sharding import PartitionSpec as P

adapter_scale = 2.0
most = 2
lanes = 128
block = 16
ahead = 8
bf16 = jnp.bfloat16
f32 = jnp.float32
i32 = jnp.int32


def iota(shape, axis):
    return lax.broadcasted_iota(i32, shape, axis)


def one_hot(hit):
    return jnp.where(hit, 1.0, 0.0).astype(bf16)


def times(a, b):
    return jnp.dot(a, b, preferred_element_type=f32)


def column_of(row):
    size = row.shape[1]
    square = (size, size)
    return jnp.sum(jnp.where(iota(square, 0) == iota(square, 1), row, 0), axis=1, keepdims=True)


def place_rows(present, requested_ref, slot_ref):
    group = lax.axis_index("replica")
    owners = requested_ref.shape[0]
    count = slot_ref.shape[1]
    mine = iota(requested_ref.shape, 0) == group
    entries = jnp.sum(jnp.where(mine, requested_ref[...], 0), axis=0, keepdims=True)
    named = iota((owners, count), 0) == slot_ref[...]
    before = one_hot(iota((count, count), 0) < iota((count, count), 1))
    earlier = times(one_hot(named), before)
    place = jnp.sum(jnp.where(named, earlier, 0.0), axis=0, keepdims=True)
    owner = lax.div(entries, jnp.int32(present)).astype(f32).astype(bf16)
    owner = times(jnp.broadcast_to(owner, (block, owners)), one_hot(named))[:1]
    return (owner * float(most) + place).astype(i32)


def send_kernel(present, requested_ref, slot_ref, attention_ref, sent_ref, goes_ref):
    goes = place_rows(present, requested_ref, slot_ref)
    count, features = attention_ref.shape
    chunks = features // lanes
    goes_ref[...] = goes
    target = jnp.concatenate([goes * chunks + k for k in range(chunks)], axis=1)
    stacked = jnp.concatenate(
        [attention_ref[:, k * lanes : (k + 1) * lanes] for k in range(chunks)], axis=0
    )
    pick = one_hot(iota((sent_ref.shape[0], chunks * count), 0) == target)
    sent_ref[...] = times(pick, stacked).astype(bf16)


def base_kernel(
    attention_ref, weight_ref, mine_ref, other_ref, rows, weights, arrived
):
    chips, _, columns = mine_ref.shape
    index = lax.axis_index("tensor")
    core = lax.rem(index, 2)
    chip = lax.div(index, 2)

    def fetch(slot):
        away = (0, 2, 1, 3)[slot // 2]
        device = 2 * (chip ^ away) + (core if slot % 2 else 1 - core)
        start = pl.multiple_of(device * columns, columns)
        return pltpu.make_async_copy(
            weight_ref.at[:, pl.ds(start, columns)], weights.at[slot], arrived.at[slot]
        )

    load = pltpu.make_async_copy(attention_ref, rows, arrived.at[2 * chips])
    load.start()
    for slot in range(ahead):
        fetch(slot).start()
    load.wait()
    for slot in range(2 * chips):
        fetch(slot).wait()
        if slot + ahead < 2 * chips:
            fetch(slot + ahead).start()
        base = times(rows[...], weights[slot])
        if slot % 2:
            mine_ref[slot // 2] = base
        else:
            other_ref[slot // 2] = base.astype(bf16)


def chip_kernel(mine_ref, got_ref, near_ref, far_ref):
    half = near_ref.shape[0]
    near_ref[...] = mine_ref[:half] + got_ref[:half].astype(f32)
    far_ref[...] = (mine_ref[half:] + got_ref[half:].astype(f32)).astype(bf16)


def pair_kernel(goes_ref, near_ref, got_ref, mine_ref, send_ref, pick_ref):
    mine_ref[...] = near_ref[0] + got_ref[0].astype(f32)
    send_ref[...] = (near_ref[1] + got_ref[1].astype(f32)).astype(bf16)
    rows, columns = mine_ref.shape
    chunks = columns // lanes
    goes = column_of(goes_ref[...]) * chunks
    for k in range(chunks):
        pick_ref[k * rows : (k + 1) * rows, :] = one_hot(
            iota((rows, pick_ref.shape[1]), 1) == goes + k
        )


def named_here(requested_ref, present):
    owner = lax.axis_index("replica")
    requested = requested_ref[...]
    mine = lax.div(requested, jnp.int32(present)) == owner
    return jnp.sum(
        jnp.where(mine, lax.rem(requested, jnp.int32(present)), 0), axis=1, keepdims=True
    )


def interleave(parts, backward):
    shape = (parts * block, parts * block)
    row, column = iota(shape, 0), iota(shape, 1)
    if backward:
        row, column = column, row
    return one_hot(lax.rem(row, jnp.int32(parts)) * block + lax.div(row, jnp.int32(parts)) == column)


def low_kernel(requested_ref, here_ref, down_ref, up_ref, out_ref, rows_ref):
    present, rank, features = down_ref.shape
    groups = requested_ref.shape[0]
    chunks = features // lanes
    parts = most * chunks
    order = interleave(parts, True)
    for b in range(groups // block):
        rows = times(order, here_ref[b * parts * block : (b + 1) * parts * block, :]).astype(bf16)
        for j in range(parts):
            place, k = divmod(j, chunks)
            rows_ref[
                place * groups + b * block : place * groups + (b + 1) * block,
                k * lanes : (k + 1) * lanes,
            ] = rows[j * block : (j + 1) * block, :]
    down = jnp.concatenate([down_ref[a] for a in range(present)], axis=0)
    low = lax.dot_general(
        rows_ref[...], down, (((1,), (1,)), ((), ())), preferred_element_type=f32
    )
    which = named_here(requested_ref, present)
    places = []
    for place in range(most):
        one = low[place * groups : (place + 1) * groups, :]
        places.append(
            sum(
                jnp.where(which == a, one[:, a * rank : (a + 1) * rank], 0.0)
                for a in range(present)
            )
        )
    low = jnp.concatenate(places, axis=1).astype(bf16)
    up = jnp.concatenate([up_ref[a] for a in range(present)], axis=0)
    height = up.shape[0]
    shards = out_ref.shape[0]
    columns = up.shape[1] // shards
    for peer in range(shards):
        for k in range(columns // lanes):
            out_ref[peer, k * height : (k + 1) * height, :] = up[
                :, peer * columns + k * lanes : peer * columns + (k + 1) * lanes
            ]
        out_ref[peer, out_ref.shape[1] - groups :, :] = low


def result_kernel(present, requested_ref, low_ref, up_ref, out_ref, rows_ref):
    shards, groups, width = low_ref.shape
    rank = width // most
    window = rank // shards
    depth = shards * present * window
    chunks = up_ref.shape[1] // (present * window)
    parts = most * chunks
    low = low_ref[0].astype(f32)
    for peer in range(1, shards):
        low = low + low_ref[peer].astype(f32)
    low = (adapter_scale * low).astype(bf16)
    up = jnp.concatenate(
        [
            jnp.concatenate(
                [up_ref[peer, k * present * window : (k + 1) * present * window, :] for peer in range(shards)],
                axis=0,
            )
            for k in range(chunks)
        ],
        axis=1,
    )
    which = named_here(requested_ref, present)
    source, target = iota((width, depth), 0), iota((width, depth), 1)
    shard = lax.div(target, jnp.int32(present * window))
    rank_of = shard * window + lax.rem(target, jnp.int32(window))
    adapter = iota((groups, depth), 1)
    adapter = lax.rem(lax.div(adapter, jnp.int32(window)), jnp.int32(present))
    order = interleave(parts, False)
    results = []
    for place in range(most):
        spread = times(low, one_hot(source == place * rank + rank_of)).astype(bf16)
        spread = jnp.where(adapter == which, spread, jnp.zeros_like(spread))
        results.append(times(spread, up).astype(bf16))
    for b in range(groups // block):
        for j in range(parts):
            place, k = divmod(j, chunks)
            rows_ref[j * block : (j + 1) * block, :] = results[place][
                b * block : (b + 1) * block, k * lanes : (k + 1) * lanes
            ]
        out_ref[b * parts * block : (b + 1) * parts * block, :] = times(order, rows_ref[...]).astype(bf16)


def lora_kernel(pick_ref, back_ref, out_ref):
    rows, columns = out_ref.shape
    mine = times(pick_ref[...], back_ref[...])
    for k in range(columns // lanes):
        out_ref[:, k * lanes : (k + 1) * lanes] = mine[k * rows : (k + 1) * rows, :]


def finish_kernel(lora_ref, mine_ref, got_ref, out_ref):
    out_ref[...] = (mine_ref[...] + got_ref[...].astype(f32) + lora_ref[...]).astype(bf16)


def whole(shape):
    return pl.BlockSpec(shape, lambda *_: (0,) * len(shape))


def call(kernel, out_shape, in_specs, out_specs, cost=(0, 0), limit=4, **options):
    return pl.pallas_call(
        kernel,
        grid=(1,),
        out_shape=out_shape,
        in_specs=in_specs,
        out_specs=out_specs,
        compiler_params=pltpu.CompilerParams(vmem_limit_bytes=limit << 20),
        cost_estimate=pl.CostEstimate(flops=cost[0], bytes_accessed=cost[1], transcendentals=0),
        **options,
    )


def local(attention, weight, down, up, requested, slot):
    rows, features = attention.shape
    present, rank, _ = down.shape
    window = up.shape[1]
    groups = requested.shape[0]
    shards = lax.axis_size("tensor")
    columns = weight.shape[1] // shards
    parts = most * features // lanes
    out_parts = most * columns // lanes
    chunks = columns // lanes
    shape = jax.ShapeDtypeStruct

    sent, goes = call(
        functools.partial(send_kernel, present),
        (shape((groups * parts, lanes), bf16), shape((1, rows), i32)),
        [whole(requested.shape), whole((1, rows)), whole(attention.shape)],
        (whole((groups * parts, lanes)), whole((1, rows))),
        cost=(1 << 34, 1 << 20),
        limit=56,
    )(requested, slot.reshape(1, rows), attention)
    here = lax.all_to_all(sent.reshape(groups, parts, lanes), "replica", 0, 0, tiled=True)

    chips = shards // 2
    tile = (rows, columns)
    mine, other = call(
        base_kernel,
        (shape((chips,) + tile, f32), shape((chips,) + tile, bf16)),
        [pl.BlockSpec(memory_space=pl.ANY), pl.BlockSpec(memory_space=pl.ANY)],
        (whole((chips,) + tile), whole((chips,) + tile)),
        cost=(1 << 34, 1 << 20),
        limit=51,
        scratch_shapes=[
            pltpu.VMEM((rows, features), bf16),
            pltpu.VMEM((shards, features, columns), bf16),
            pltpu.SemaphoreType.DMA((shards + 1,)),
        ],
    )(attention, weight)
    got = lax.ppermute(other, "tensor", [(i, i ^ 1) for i in range(shards)])

    up_rows = chunks * present * window
    message = call(
        low_kernel,
        shape((shards, up_rows + groups, lanes), bf16),
        [whole(requested.shape), whole((groups * parts, lanes)), whole(down.shape), whole(up.shape)],
        whole((shards, up_rows + groups, lanes)),
        cost=(6 * groups * parts * lanes * lanes, 6 * groups * parts * lanes),
        scratch_shapes=[pltpu.VMEM((most * groups, features), bf16)],
    )(requested, here.reshape(groups * parts, lanes), down, up)
    message = lax.all_to_all(message, "tensor", 0, 0, tiled=True)

    near, far = call(
        chip_kernel,
        (shape((chips // 2,) + tile, f32), shape((chips // 2,) + tile, bf16)),
        [whole((chips,) + tile), whole((chips,) + tile)],
        (whole((chips // 2,) + tile), whole((chips // 2,) + tile)),
        cost=(1 << 34, 1 << 20),
    )(mine, got)
    got = lax.ppermute(far, "tensor", [(i, i ^ 2) for i in range(shards)])

    result = call(
        functools.partial(result_kernel, present),
        shape((groups * out_parts, lanes), bf16),
        [
            whole(requested.shape),
            pl.BlockSpec((shards, groups, lanes), lambda *_: (0, up_rows // groups, 0)),
            pl.BlockSpec((shards, up_rows, lanes), lambda *_: (0, 0, 0)),
        ],
        whole((groups * out_parts, lanes)),
        cost=(6 * groups * parts * lanes * lanes, 6 * groups * parts * lanes),
        scratch_shapes=[pltpu.VMEM((out_parts * block, lanes), bf16)],
    )(requested, message, message)
    back = lax.all_to_all(result.reshape(groups, out_parts, lanes), "replica", 0, 0, tiled=True)

    mine, send, pick = call(
        pair_kernel,
        (shape(tile, f32), shape(tile, bf16), shape((chunks * rows, groups * out_parts), bf16)),
        [whole((1, rows)), whole((chips // 2,) + tile), whole((chips // 2,) + tile)],
        (whole(tile), whole(tile), whole((chunks * rows, groups * out_parts))),
        cost=(1 << 34, 1 << 20),
    )(goes, near, got)
    got = lax.ppermute(send, "tensor", [(i, i ^ 4) for i in range(shards)])

    lora = call(
        lora_kernel,
        shape(tile, f32),
        [whole((chunks * rows, groups * out_parts)), whole((groups * out_parts, lanes))],
        whole(tile),
        cost=(2 * chunks * rows * groups * out_parts * lanes, 4 * chunks * rows * groups * out_parts),
    )(pick, back.reshape(groups * out_parts, lanes))
    return call(
        finish_kernel,
        shape(tile, bf16),
        [whole(tile), whole(tile), whole(tile)],
        whole(tile),
    )(lora, mine, got)


def solution(mesh):
    in_specs = (
        P("replica", "tensor"),
        P("tensor", None),
        P("replica", None, "tensor"),
        P("replica", "tensor", None),
        P(),
        P("replica", None),
    )
    out_specs = P("replica", "tensor")
    return jax.shard_map(local, mesh=mesh, in_specs=in_specs, out_specs=out_specs, check_vma=False)
```

```python
import functools
import math

import jax
import jax.numpy as jnp
from jax import lax
from jax.experimental import pallas as pl
from jax.experimental.pallas import tpu as pltpu
from jax.sharding import PartitionSpec as P

adapter_scale = 2.0
most = 2
lanes = 128
block = 16
first_z, first_y = 6, 4
ahead = 8
bf16 = jnp.bfloat16
f32 = jnp.float32
i32 = jnp.int32


def iota(shape, axis):
    return lax.broadcasted_iota(i32, shape, axis)


def one_hot(hit):
    return jnp.where(hit, 1.0, 0.0).astype(bf16)


def times(a, b):
    return jnp.dot(a, b, preferred_element_type=f32)


def ring_order(count):
    side = math.isqrt(count)
    if side * side != count:
        return list(range(count))
    return [
        (first_z + z) % side * side + (first_y + y) % side for z in range(side) for y in range(side)
    ]


def place_in_order(device, count):
    side = math.isqrt(count)
    if side * side != count:
        return device
    z, y = lax.div(device, jnp.int32(side)), lax.rem(device, jnp.int32(side))
    z = lax.rem(z + (side - first_z % side), jnp.int32(side))
    return z * side + lax.rem(y + (side - first_y % side), jnp.int32(side))


def column_of(row):
    size = row.shape[1]
    square = (size, size)
    return jnp.sum(jnp.where(iota(square, 0) == iota(square, 1), row, 0), axis=1, keepdims=True)


def place_rows(present, requested_ref, slot_ref):
    group = lax.axis_index("replica")
    owners = requested_ref.shape[0]
    count = slot_ref.shape[1]
    mine = iota(requested_ref.shape, 0) == group
    entries = jnp.sum(jnp.where(mine, requested_ref[...], 0), axis=0, keepdims=True)
    named = iota((owners, count), 0) == slot_ref[...]
    before = one_hot(iota((count, count), 0) < iota((count, count), 1))
    earlier = times(one_hot(named), before)
    place = jnp.sum(jnp.where(named, earlier, 0.0), axis=0, keepdims=True)
    owner = place_in_order(lax.div(entries, jnp.int32(present)), owners).astype(f32).astype(bf16)
    owner = times(jnp.broadcast_to(owner, (block, owners)), one_hot(named))[:1]
    return (owner * float(most) + place).astype(i32)


def send_kernel(present, requested_ref, slot_ref, attention_ref, sent_ref, goes_ref):
    goes = place_rows(present, requested_ref, slot_ref)
    count, features = attention_ref.shape
    chunks = features // lanes
    goes_ref[...] = goes
    target = jnp.concatenate([goes * chunks + k for k in range(chunks)], axis=1)
    stacked = jnp.concatenate(
        [attention_ref[:, k * lanes : (k + 1) * lanes] for k in range(chunks)], axis=0
    )
    pick = one_hot(iota((sent_ref.shape[0], chunks * count), 0) == target)
    sent_ref[...] = times(pick, stacked).astype(bf16)


def base_kernel(
    present,
    requested_ref,
    attention_ref,
    weight_ref,
    mine_ref,
    other_ref,
    which_ref,
    rows,
    weights,
    arrived,
):
    chips, _, columns = mine_ref.shape
    index = lax.axis_index("tensor")
    core = lax.rem(index, 2)
    chip = lax.div(index, 2)

    def fetch(slot):
        away = slot // 2
        device = 2 * (chip ^ away) + (core if slot % 2 else 1 - core)
        start = pl.multiple_of(device * columns, columns)
        return pltpu.make_async_copy(
            weight_ref.at[:, pl.ds(start, columns)], weights.at[slot], arrived.at[slot]
        )

    load = pltpu.make_async_copy(attention_ref, rows, arrived.at[2 * chips])
    load.start()
    for slot in range(ahead):
        fetch(slot).start()
    which_ref[...] = named_here(requested_ref, present)
    load.wait()
    for slot in range(2 * chips):
        fetch(slot).wait()
        if slot + ahead < 2 * chips:
            fetch(slot + ahead).start()
        base = times(rows[...], weights[slot])
        if slot % 2:
            mine_ref[slot // 2] = base
        else:
            other_ref[slot // 2] = base.astype(bf16)


def chip_kernel(mine_ref, got_ref, near_ref, far_ref):
    half = near_ref.shape[0]
    near_ref[...] = mine_ref[:half] + got_ref[:half].astype(f32)
    far_ref[...] = (mine_ref[half:] + got_ref[half:].astype(f32)).astype(bf16)


def pair_kernel(goes_ref, near_ref, got_ref, mine_ref, send_ref, pick_ref):
    mine_ref[...] = near_ref[0] + got_ref[0].astype(f32)
    send_ref[...] = (near_ref[1] + got_ref[1].astype(f32)).astype(bf16)
    rows, columns = mine_ref.shape
    chunks = columns // lanes
    goes = column_of(goes_ref[...]) * chunks
    for k in range(chunks):
        pick_ref[k * rows : (k + 1) * rows, :] = one_hot(
            iota((rows, pick_ref.shape[1]), 1) == goes + k
        )


def named_here(requested_ref, present):
    owner = lax.axis_index("replica")
    requested = requested_ref[...]
    groups = requested.shape[0]
    mine = lax.div(requested, jnp.int32(present)) == owner
    which = jnp.sum(
        jnp.where(mine, lax.rem(requested, jnp.int32(present)), 0), axis=1, keepdims=True
    )
    placed = iota((groups, groups), 1) == place_in_order(iota((groups, groups), 0), groups)
    which = jnp.sum(jnp.where(placed, which, 0), axis=0, keepdims=True)
    return column_of(which)


def interleave(parts, backward):
    shape = (parts * block, parts * block)
    row, column = iota(shape, 0), iota(shape, 1)
    if backward:
        row, column = column, row
    return one_hot(lax.rem(row, jnp.int32(parts)) * block + lax.div(row, jnp.int32(parts)) == column)


def low_kernel(which_ref, here_ref, down_ref, up_ref, out_ref, rows_ref):
    present, rank, features = down_ref.shape
    groups = which_ref.shape[0]
    chunks = features // lanes
    parts = most * chunks
    order = interleave(parts, True)
    for b in range(groups // block):
        rows = times(order, here_ref[b * parts * block : (b + 1) * parts * block, :]).astype(bf16)
        for j in range(parts):
            place, k = divmod(j, chunks)
            rows_ref[
                place * groups + b * block : place * groups + (b + 1) * block,
                k * lanes : (k + 1) * lanes,
            ] = rows[j * block : (j + 1) * block, :]
    down = jnp.concatenate([down_ref[a] for a in range(present)], axis=0)
    low = lax.dot_general(
        rows_ref[...], down, (((1,), (1,)), ((), ())), preferred_element_type=f32
    )
    which = which_ref[...]
    places = []
    for place in range(most):
        one = low[place * groups : (place + 1) * groups, :]
        places.append(
            sum(
                jnp.where(which == a, one[:, a * rank : (a + 1) * rank], 0.0)
                for a in range(present)
            )
        )
    low = jnp.concatenate(places, axis=1).astype(bf16)
    up = jnp.concatenate([up_ref[a] for a in range(present)], axis=0)
    height = up.shape[0]
    shards = out_ref.shape[0]
    columns = up.shape[1] // shards
    for peer in range(shards):
        for k in range(columns // lanes):
            out_ref[peer, k * height : (k + 1) * height, :] = up[
                :, peer * columns + k * lanes : peer * columns + (k + 1) * lanes
            ]
        out_ref[peer, out_ref.shape[1] - groups :, :] = low


def result_kernel(present, which_ref, low_ref, up_ref, out_ref, rows_ref):
    shards, groups, width = low_ref.shape
    rank = width // most
    window = rank // shards
    depth = shards * present * window
    chunks = up_ref.shape[1] // (present * window)
    parts = most * chunks
    low = low_ref[0].astype(f32)
    for peer in range(1, shards):
        low = low + low_ref[peer].astype(f32)
    low = (adapter_scale * low).astype(bf16)
    up = jnp.concatenate(
        [
            jnp.concatenate(
                [up_ref[peer, k * present * window : (k + 1) * present * window, :] for peer in range(shards)],
                axis=0,
            )
            for k in range(chunks)
        ],
        axis=1,
    )
    which = which_ref[...]
    source, target = iota((width, depth), 0), iota((width, depth), 1)
    shard = lax.div(target, jnp.int32(present * window))
    rank_of = shard * window + lax.rem(target, jnp.int32(window))
    adapter = iota((groups, depth), 1)
    adapter = lax.rem(lax.div(adapter, jnp.int32(window)), jnp.int32(present))
    order = interleave(parts, False)
    results = []
    for place in range(most):
        spread = times(low, one_hot(source == place * rank + rank_of)).astype(bf16)
        spread = jnp.where(adapter == which, spread, jnp.zeros_like(spread))
        results.append(times(spread, up).astype(bf16))
    for b in range(groups // block):
        for j in range(parts):
            place, k = divmod(j, chunks)
            rows_ref[j * block : (j + 1) * block, :] = results[place][
                b * block : (b + 1) * block, k * lanes : (k + 1) * lanes
            ]
        out_ref[b * parts * block : (b + 1) * parts * block, :] = times(order, rows_ref[...]).astype(bf16)


def lora_kernel(pick_ref, back_ref, out_ref):
    rows, columns = out_ref.shape
    mine = times(pick_ref[...], back_ref[...])
    for k in range(columns // lanes):
        out_ref[:, k * lanes : (k + 1) * lanes] = mine[k * rows : (k + 1) * rows, :]


def finish_kernel(lora_ref, mine_ref, got_ref, out_ref):
    out_ref[...] = (mine_ref[...] + got_ref[...].astype(f32) + lora_ref[...]).astype(bf16)


def whole(shape):
    return pl.BlockSpec(shape, lambda *_: (0,) * len(shape))


def call(kernel, out_shape, in_specs, out_specs, cost=(0, 0), limit=4, **options):
    return pl.pallas_call(
        kernel,
        grid=(1,),
        out_shape=out_shape,
        in_specs=in_specs,
        out_specs=out_specs,
        compiler_params=pltpu.CompilerParams(vmem_limit_bytes=limit << 20),
        cost_estimate=pl.CostEstimate(flops=cost[0], bytes_accessed=cost[1], transcendentals=0),
        **options,
    )


def local(attention, weight, down, up, requested, slot):
    rows, features = attention.shape
    present, rank, _ = down.shape
    window = up.shape[1]
    groups = requested.shape[0]
    shards = lax.axis_size("tensor")
    columns = weight.shape[1] // shards
    parts = most * features // lanes
    out_parts = most * columns // lanes
    chunks = columns // lanes
    shape = jax.ShapeDtypeStruct
    order = [ring_order(groups)]

    sent, goes = call(
        functools.partial(send_kernel, present),
        (shape((groups * parts, lanes), bf16), shape((1, rows), i32)),
        [whole(requested.shape), whole((1, rows)), whole(attention.shape)],
        (whole((groups * parts, lanes)), whole((1, rows))),
        cost=(1 << 34, 1 << 20),
        limit=56,
    )(requested, slot.reshape(1, rows), attention)
    here = lax.all_to_all(sent.reshape(groups, parts, lanes), "replica", 0, 0, axis_index_groups=order, tiled=True)

    chips = shards // 2
    tile = (rows, columns)
    mine, other, which = call(
        functools.partial(base_kernel, present),
        (shape((chips,) + tile, f32), shape((chips,) + tile, bf16), shape((groups, 1), i32)),
        [
            whole(requested.shape),
            pl.BlockSpec(memory_space=pl.ANY),
            pl.BlockSpec(memory_space=pl.ANY),
        ],
        (whole((chips,) + tile), whole((chips,) + tile), whole((groups, 1))),
        cost=(1 << 34, 1 << 20),
        limit=51,
        scratch_shapes=[
            pltpu.VMEM((rows, features), bf16),
            pltpu.VMEM((shards, features, columns), bf16),
            pltpu.SemaphoreType.DMA((shards + 1,)),
        ],
    )(requested, attention, weight)
    got = lax.ppermute(other, "tensor", [(i, i ^ 1) for i in range(shards)])

    up_rows = chunks * present * window
    message = call(
        low_kernel,
        shape((shards, up_rows + groups, lanes), bf16),
        [whole((groups, 1)), whole((groups * parts, lanes)), whole(down.shape), whole(up.shape)],
        whole((shards, up_rows + groups, lanes)),
        cost=(6 * groups * parts * lanes * lanes, 6 * groups * parts * lanes),
        scratch_shapes=[pltpu.VMEM((most * groups, features), bf16)],
    )(which, here.reshape(groups * parts, lanes), down, up)
    message = lax.all_to_all(message, "tensor", 0, 0, tiled=True)

    near, far = call(
        chip_kernel,
        (shape((chips // 2,) + tile, f32), shape((chips // 2,) + tile, bf16)),
        [whole((chips,) + tile), whole((chips,) + tile)],
        (whole((chips // 2,) + tile), whole((chips // 2,) + tile)),
        cost=(1 << 34, 1 << 20),
    )(mine, got)
    got = lax.ppermute(far, "tensor", [(i, i ^ 4) for i in range(shards)])

    result = call(
        functools.partial(result_kernel, present),
        shape((groups * out_parts, lanes), bf16),
        [
            whole((groups, 1)),
            pl.BlockSpec((shards, groups, lanes), lambda *_: (0, up_rows // groups, 0)),
            pl.BlockSpec((shards, up_rows, lanes), lambda *_: (0, 0, 0)),
        ],
        whole((groups * out_parts, lanes)),
        cost=(6 * groups * parts * lanes * lanes, 6 * groups * parts * lanes),
        scratch_shapes=[pltpu.VMEM((out_parts * block, lanes), bf16)],
    )(which, message, message)
    back = lax.all_to_all(result.reshape(groups, out_parts, lanes), "replica", 0, 0, axis_index_groups=order, tiled=True)

    mine, send, pick = call(
        pair_kernel,
        (shape(tile, f32), shape(tile, bf16), shape((chunks * rows, groups * out_parts), bf16)),
        [whole((1, rows)), whole((chips // 2,) + tile), whole((chips // 2,) + tile)],
        (whole(tile), whole(tile), whole((chunks * rows, groups * out_parts))),
        cost=(1 << 34, 1 << 20),
    )(goes, near, got)
    got = lax.ppermute(send, "tensor", [(i, i ^ 2) for i in range(shards)])

    lora = call(
        lora_kernel,
        shape(tile, f32),
        [whole((chunks * rows, groups * out_parts)), whole((groups * out_parts, lanes))],
        whole(tile),
        cost=(2 * chunks * rows * groups * out_parts * lanes, 4 * chunks * rows * groups * out_parts),
    )(pick, back.reshape(groups * out_parts, lanes))
    return call(
        finish_kernel,
        shape(tile, bf16),
        [whole(tile), whole(tile), whole(tile)],
        whole(tile),
    )(lora, mine, got)


def solution(mesh):
    in_specs = (
        P("replica", "tensor"),
        P("tensor", None),
        P("replica", None, "tensor"),
        P("replica", "tensor", None),
        P(),
        P("replica", None),
    )
    out_specs = P("replica", "tensor")
    return jax.shard_map(local, mesh=mesh, in_specs=in_specs, out_specs=out_specs, check_vma=False)
```

```python
import functools
import math

import jax
import jax.numpy as jnp
from jax import lax
from jax.experimental import pallas as pl
from jax.experimental.pallas import tpu as pltpu
from jax.sharding import PartitionSpec as P

adapter_scale = 2.0
most = 2
lanes = 128
block = 16
first_z, first_y = 6, 4
bf16 = jnp.bfloat16
f32 = jnp.float32
i32 = jnp.int32


def iota(shape, axis):
    return lax.broadcasted_iota(i32, shape, axis)


def one_hot(hit):
    return jnp.where(hit, 1.0, 0.0).astype(bf16)


def times(a, b):
    return jnp.dot(a, b, preferred_element_type=f32)


def steps_of(side):
    return [0] + sorted(range(1, side), key=lambda step: -min(step, side - step))


def ring_order(count):
    side = math.isqrt(count)
    if side * side != count:
        return list(range(count))
    steps = steps_of(side)
    return [(first_z + z) % side * side + (first_y + y) % side for z in steps for y in steps]


def place_in_order(device, count):
    side = math.isqrt(count)
    if side * side != count:
        return device

    def place(position, first):
        step = lax.rem(position + (side - first % side), jnp.int32(side))
        return sum(jnp.where(step == one, n, 0) for n, one in enumerate(steps_of(side)))

    z = place(lax.div(device, jnp.int32(side)), first_z)
    return z * side + place(lax.rem(device, jnp.int32(side)), first_y)


def column_of(row):
    size = row.shape[1]
    square = (size, size)
    return jnp.sum(jnp.where(iota(square, 0) == iota(square, 1), row, 0), axis=1, keepdims=True)


def place_rows(present, requested_ref, slot_ref):
    group = lax.axis_index("replica")
    owners = requested_ref.shape[0]
    count = slot_ref.shape[1]
    mine = iota(requested_ref.shape, 0) == group
    entries = jnp.sum(jnp.where(mine, requested_ref[...], 0), axis=0, keepdims=True)
    named = iota((owners, count), 0) == slot_ref[...]
    before = one_hot(iota((count, count), 0) < iota((count, count), 1))
    earlier = times(one_hot(named), before)
    place = jnp.sum(jnp.where(named, earlier, 0.0), axis=0, keepdims=True)
    owner = place_in_order(lax.div(entries, jnp.int32(present)), owners).astype(f32).astype(bf16)
    owner = times(jnp.broadcast_to(owner, (block, owners)), one_hot(named))[:1]
    return (owner * float(most) + place).astype(i32)


def send_kernel(present, requested_ref, slot_ref, attention_ref, sent_ref, goes_ref):
    goes = place_rows(present, requested_ref, slot_ref)
    count, features = attention_ref.shape
    chunks = features // lanes
    goes_ref[...] = goes
    target = jnp.concatenate([goes * chunks + k for k in range(chunks)], axis=1)
    stacked = jnp.concatenate(
        [attention_ref[:, k * lanes : (k + 1) * lanes] for k in range(chunks)], axis=0
    )
    pick = one_hot(iota((sent_ref.shape[0], chunks * count), 0) == target)
    sent_ref[...] = times(pick, stacked).astype(bf16)


def fetches(weight_ref, weights, arrived, other_core):
    chips, _, columns = weights.shape
    index = lax.axis_index("tensor")
    core = lax.rem(index, 2)
    chip = lax.div(index, 2)
    copies = []
    for away in range(chips):
        device = 2 * (chip ^ away) + (1 - core if other_core else core)
        start = pl.multiple_of(device * columns, columns)
        copies.append(
            pltpu.make_async_copy(
                weight_ref.at[:, pl.ds(start, columns)], weights.at[away], arrived.at[away]
            )
        )
    return copies


def other_kernel(
    present, requested_ref, attention_ref, weight_ref, other_ref, which_ref, rows, weights, arrived
):
    load = pltpu.make_async_copy(attention_ref, rows, arrived.at[weights.shape[0]])
    load.start()
    copies = fetches(weight_ref, weights, arrived, True)
    for copy in copies:
        copy.start()
    which_ref[...] = named_here(requested_ref, present)
    load.wait()
    for away, copy in enumerate(copies):
        copy.wait()
        other_ref[away] = times(rows[...], weights[away]).astype(bf16)


def chip_kernel(attention_ref, weight_ref, got_ref, near_ref, far_ref, rows, weights, arrived):
    load = pltpu.make_async_copy(attention_ref, rows, arrived.at[weights.shape[0]])
    load.start()
    copies = fetches(weight_ref, weights, arrived, False)
    for copy in copies:
        copy.start()
    load.wait()
    half = near_ref.shape[0]
    for away, copy in enumerate(copies):
        copy.wait()
        total = times(rows[...], weights[away]) + got_ref[away].astype(f32)
        if away < half:
            near_ref[away] = total
        else:
            far_ref[away - half] = total.astype(bf16)


def pair_kernel(goes_ref, near_ref, got_ref, mine_ref, send_ref, pick_ref):
    mine_ref[...] = near_ref[0] + got_ref[0].astype(f32)
    send_ref[...] = (near_ref[1] + got_ref[1].astype(f32)).astype(bf16)
    rows, columns = mine_ref.shape
    chunks = columns // lanes
    goes = column_of(goes_ref[...]) * chunks
    for k in range(chunks):
        pick_ref[k * rows : (k + 1) * rows, :] = one_hot(
            iota((rows, pick_ref.shape[1]), 1) == goes + k
        )


def named_here(requested_ref, present):
    owner = lax.axis_index("replica")
    requested = requested_ref[...]
    groups = requested.shape[0]
    mine = lax.div(requested, jnp.int32(present)) == owner
    which = jnp.sum(
        jnp.where(mine, lax.rem(requested, jnp.int32(present)), 0), axis=1, keepdims=True
    )
    placed = iota((groups, groups), 1) == place_in_order(iota((groups, groups), 0), groups)
    which = jnp.sum(jnp.where(placed, which, 0), axis=0, keepdims=True)
    return column_of(which)


def interleave(parts, backward):
    shape = (parts * block, parts * block)
    row, column = iota(shape, 0), iota(shape, 1)
    if backward:
        row, column = column, row
    return one_hot(lax.rem(row, jnp.int32(parts)) * block + lax.div(row, jnp.int32(parts)) == column)


def low_kernel(which_ref, here_ref, down_ref, up_ref, out_ref, rows_ref):
    present, rank, features = down_ref.shape
    groups = which_ref.shape[0]
    chunks = features // lanes
    parts = most * chunks
    order = interleave(parts, True)
    for b in range(groups // block):
        rows = times(order, here_ref[b * parts * block : (b + 1) * parts * block, :]).astype(bf16)
        for j in range(parts):
            place, k = divmod(j, chunks)
            rows_ref[
                place * groups + b * block : place * groups + (b + 1) * block,
                k * lanes : (k + 1) * lanes,
            ] = rows[j * block : (j + 1) * block, :]
    down = jnp.concatenate([down_ref[a] for a in range(present)], axis=0)
    low = lax.dot_general(
        rows_ref[...], down, (((1,), (1,)), ((), ())), preferred_element_type=f32
    )
    which = which_ref[...]
    places = []
    for place in range(most):
        one = low[place * groups : (place + 1) * groups, :]
        places.append(
            sum(
                jnp.where(which == a, one[:, a * rank : (a + 1) * rank], 0.0)
                for a in range(present)
            )
        )
    low = jnp.concatenate(places, axis=1).astype(bf16)
    up = jnp.concatenate([up_ref[a] for a in range(present)], axis=0)
    height = up.shape[0]
    shards = out_ref.shape[0]
    columns = up.shape[1] // shards
    for peer in range(shards):
        for k in range(columns // lanes):
            out_ref[peer, k * height : (k + 1) * height, :] = up[
                :, peer * columns + k * lanes : peer * columns + (k + 1) * lanes
            ]
        out_ref[peer, out_ref.shape[1] - groups :, :] = low


def result_kernel(present, which_ref, low_ref, up_ref, out_ref, rows_ref):
    shards, groups, width = low_ref.shape
    rank = width // most
    window = rank // shards
    depth = shards * present * window
    chunks = up_ref.shape[1] // (present * window)
    parts = most * chunks
    low = low_ref[0].astype(f32)
    for peer in range(1, shards):
        low = low + low_ref[peer].astype(f32)
    low = (adapter_scale * low).astype(bf16)
    up = jnp.concatenate(
        [
            jnp.concatenate(
                [up_ref[peer, k * present * window : (k + 1) * present * window, :] for peer in range(shards)],
                axis=0,
            )
            for k in range(chunks)
        ],
        axis=1,
    )
    which = which_ref[...]
    source, target = iota((width, depth), 0), iota((width, depth), 1)
    shard = lax.div(target, jnp.int32(present * window))
    rank_of = shard * window + lax.rem(target, jnp.int32(window))
    adapter = iota((groups, depth), 1)
    adapter = lax.rem(lax.div(adapter, jnp.int32(window)), jnp.int32(present))
    order = interleave(parts, False)
    spread = times(
        low,
        jnp.concatenate([one_hot(source == place * rank + rank_of) for place in range(most)], axis=1),
    ).astype(bf16)
    spread = jnp.concatenate(
        [
            jnp.where(adapter == which, spread[:, place * depth : (place + 1) * depth], jnp.zeros((), bf16))
            for place in range(most)
        ],
        axis=0,
    )
    results = times(spread, up).astype(bf16)
    for b in range(groups // block):
        for j in range(parts):
            place, k = divmod(j, chunks)
            start = place * groups + b * block
            rows_ref[j * block : (j + 1) * block, :] = results[
                start : start + block, k * lanes : (k + 1) * lanes
            ]
        out_ref[b * parts * block : (b + 1) * parts * block, :] = times(order, rows_ref[...]).astype(bf16)


def lora_kernel(pick_ref, back_ref, out_ref):
    rows, columns = out_ref.shape
    mine = times(pick_ref[...], back_ref[...])
    for k in range(columns // lanes):
        out_ref[:, k * lanes : (k + 1) * lanes] = mine[k * rows : (k + 1) * rows, :]


def finish_kernel(lora_ref, mine_ref, got_ref, out_ref):
    out_ref[...] = (mine_ref[...] + got_ref[...].astype(f32) + lora_ref[...]).astype(bf16)


def whole(shape):
    return pl.BlockSpec(shape, lambda *_: (0,) * len(shape))


def call(kernel, out_shape, in_specs, out_specs, cost=(0, 0), limit=4, **options):
    return pl.pallas_call(
        kernel,
        grid=(1,),
        out_shape=out_shape,
        in_specs=in_specs,
        out_specs=out_specs,
        compiler_params=pltpu.CompilerParams(vmem_limit_bytes=limit << 20),
        cost_estimate=pl.CostEstimate(flops=cost[0], bytes_accessed=cost[1], transcendentals=0),
        **options,
    )


def local(attention, weight, down, up, requested, slot):
    rows, features = attention.shape
    present, rank, _ = down.shape
    window = up.shape[1]
    groups = requested.shape[0]
    shards = lax.axis_size("tensor")
    columns = weight.shape[1] // shards
    parts = most * features // lanes
    out_parts = most * columns // lanes
    chunks = columns // lanes
    shape = jax.ShapeDtypeStruct
    order = [ring_order(groups)]

    sent, goes = call(
        functools.partial(send_kernel, present),
        (shape((groups * parts, lanes), bf16), shape((1, rows), i32)),
        [whole(requested.shape), whole((1, rows)), whole(attention.shape)],
        (whole((groups * parts, lanes)), whole((1, rows))),
        cost=(1 << 34, 1 << 20),
        limit=56,
    )(requested, slot.reshape(1, rows), attention)
    here = lax.all_to_all(sent.reshape(groups, parts, lanes), "replica", 0, 0, axis_index_groups=order, tiled=True)

    chips = shards // 2
    tile = (rows, columns)
    anywhere = pl.BlockSpec(memory_space=pl.ANY)
    streams = dict(
        cost=(1 << 34, 1 << 20),
        limit=51,
        scratch_shapes=[
            pltpu.VMEM((rows, features), bf16),
            pltpu.VMEM((chips, features, columns), bf16),
            pltpu.SemaphoreType.DMA((chips + 1,)),
        ],
    )
    other, which = call(
        functools.partial(other_kernel, present),
        (shape((chips,) + tile, bf16), shape((groups, 1), i32)),
        [whole(requested.shape), anywhere, anywhere],
        (whole((chips,) + tile), whole((groups, 1))),
        **streams,
    )(requested, attention, weight)
    got = lax.ppermute(other, "tensor", [(i, i ^ 1) for i in range(shards)])

    up_rows = chunks * present * window
    message = call(
        low_kernel,
        shape((shards, up_rows + groups, lanes), bf16),
        [whole((groups, 1)), whole((groups * parts, lanes)), whole(down.shape), whole(up.shape)],
        whole((shards, up_rows + groups, lanes)),
        cost=(6 * groups * parts * lanes * lanes, 6 * groups * parts * lanes),
        scratch_shapes=[pltpu.VMEM((most * groups, features), bf16)],
    )(which, here.reshape(groups * parts, lanes), down, up)
    message = lax.all_to_all(message, "tensor", 0, 0, tiled=True)

    near, far = call(
        chip_kernel,
        (shape((chips // 2,) + tile, f32), shape((chips // 2,) + tile, bf16)),
        [anywhere, anywhere, whole((chips,) + tile)],
        (whole((chips // 2,) + tile), whole((chips // 2,) + tile)),
        **streams,
    )(attention, weight, got)
    got = lax.ppermute(far, "tensor", [(i, i ^ 4) for i in range(shards)])

    result = call(
        functools.partial(result_kernel, present),
        shape((groups * out_parts, lanes), bf16),
        [
            whole((groups, 1)),
            pl.BlockSpec((shards, groups, lanes), lambda *_: (0, up_rows // groups, 0)),
            pl.BlockSpec((shards, up_rows, lanes), lambda *_: (0, 0, 0)),
        ],
        whole((groups * out_parts, lanes)),
        cost=(6 * groups * parts * lanes * lanes, 6 * groups * parts * lanes),
        scratch_shapes=[pltpu.VMEM((out_parts * block, lanes), bf16)],
    )(which, message, message)
    back = lax.all_to_all(result.reshape(groups, out_parts, lanes), "replica", 0, 0, axis_index_groups=order, tiled=True)

    mine, send, pick = call(
        pair_kernel,
        (shape(tile, f32), shape(tile, bf16), shape((chunks * rows, groups * out_parts), bf16)),
        [whole((1, rows)), whole((chips // 2,) + tile), whole((chips // 2,) + tile)],
        (whole(tile), whole(tile), whole((chunks * rows, groups * out_parts))),
        cost=(1 << 34, 1 << 20),
    )(goes, near, got)
    got = lax.ppermute(send, "tensor", [(i, i ^ 2) for i in range(shards)])

    lora = call(
        lora_kernel,
        shape(tile, f32),
        [whole((chunks * rows, groups * out_parts)), whole((groups * out_parts, lanes))],
        whole(tile),
        cost=(2 * chunks * rows * groups * out_parts * lanes, 4 * chunks * rows * groups * out_parts),
    )(pick, back.reshape(groups * out_parts, lanes))
    return call(
        finish_kernel,
        shape(tile, bf16),
        [whole(tile), whole(tile), whole(tile)],
        whole(tile),
    )(lora, mine, got)


def solution(mesh):
    in_specs = (
        P("replica", "tensor"),
        P("tensor", None),
        P("replica", None, "tensor"),
        P("replica", "tensor", None),
        P(),
        P("replica", None),
    )
    out_specs = P("replica", "tensor")
    return jax.shard_map(local, mesh=mesh, in_specs=in_specs, out_specs=out_specs, check_vma=False)
```

```python
import functools
import math

import jax
import jax.numpy as jnp
from jax import lax
from jax.experimental import pallas as pl
from jax.experimental.pallas import tpu as pltpu
from jax.sharding import PartitionSpec as P

adapter_scale = 2.0
most = 2
lanes = 128
block = 16
first_z, first_y = 6, 5
ahead = 8
bf16 = jnp.bfloat16
f32 = jnp.float32
i32 = jnp.int32


def iota(shape, axis):
    return lax.broadcasted_iota(i32, shape, axis)


def one_hot(hit):
    return jnp.where(hit, 1.0, 0.0).astype(bf16)


def times(a, b):
    return jnp.dot(a, b, preferred_element_type=f32)


def steps_of(side):
    return [0] + sorted(range(1, side), key=lambda step: -min(step, side - step))


def ring_order(count):
    side = math.isqrt(count)
    if side * side != count:
        return list(range(count))
    steps = steps_of(side)
    return [(first_z + z) % side * side + (first_y + y) % side for z in steps for y in steps]


def place_in_order(device, count):
    side = math.isqrt(count)
    if side * side != count:
        return device

    def place(position, first):
        step = lax.rem(position + (side - first % side), jnp.int32(side))
        return sum(jnp.where(step == one, n, 0) for n, one in enumerate(steps_of(side)))

    z = place(lax.div(device, jnp.int32(side)), first_z)
    return z * side + place(lax.rem(device, jnp.int32(side)), first_y)


def column_of(row):
    size = row.shape[1]
    square = (size, size)
    return jnp.sum(jnp.where(iota(square, 0) == iota(square, 1), row, 0), axis=1, keepdims=True)


def place_rows(present, requested_ref, slot_ref):
    group = lax.axis_index("replica")
    owners = requested_ref.shape[0]
    count = slot_ref.shape[1]
    mine = iota(requested_ref.shape, 0) == group
    entries = jnp.sum(jnp.where(mine, requested_ref[...], 0), axis=0, keepdims=True)
    named = iota((owners, count), 0) == slot_ref[...]
    before = one_hot(iota((count, count), 0) < iota((count, count), 1))
    earlier = times(one_hot(named), before)
    place = jnp.sum(jnp.where(named, earlier, 0.0), axis=0, keepdims=True)
    owner = place_in_order(lax.div(entries, jnp.int32(present)), owners).astype(f32).astype(bf16)
    owner = times(jnp.broadcast_to(owner, (block, owners)), one_hot(named))[:1]
    return (owner * float(most) + place).astype(i32)


def send_kernel(present, requested_ref, slot_ref, attention_ref, sent_ref, goes_ref):
    goes = place_rows(present, requested_ref, slot_ref)
    count, features = attention_ref.shape
    chunks = features // lanes
    goes_ref[...] = goes
    target = jnp.concatenate([goes * chunks + k for k in range(chunks)], axis=1)
    stacked = jnp.concatenate(
        [attention_ref[:, k * lanes : (k + 1) * lanes] for k in range(chunks)], axis=0
    )
    pick = one_hot(iota((sent_ref.shape[0], chunks * count), 0) == target)
    sent_ref[...] = times(pick, stacked).astype(bf16)


def base_kernel(
    present,
    requested_ref,
    attention_ref,
    weight_ref,
    mine_ref,
    other_ref,
    which_ref,
    rows,
    weights,
    arrived,
):
    chips, _, columns = mine_ref.shape
    index = lax.axis_index("tensor")
    core = lax.rem(index, 2)
    chip = lax.div(index, 2)

    def fetch(slot):
        away = slot // 2
        device = 2 * (chip ^ away) + (core if slot % 2 else 1 - core)
        start = pl.multiple_of(device * columns, columns)
        return pltpu.make_async_copy(
            weight_ref.at[:, pl.ds(start, columns)], weights.at[slot], arrived.at[slot]
        )

    load = pltpu.make_async_copy(attention_ref, rows, arrived.at[2 * chips])
    load.start()
    for slot in range(ahead):
        fetch(slot).start()
    which_ref[...] = named_here(requested_ref, present)
    load.wait()
    for slot in range(2 * chips):
        fetch(slot).wait()
        if slot + ahead < 2 * chips:
            fetch(slot + ahead).start()
        base = times(rows[...], weights[slot])
        if slot % 2:
            mine_ref[slot // 2] = base
        else:
            other_ref[slot // 2] = base.astype(bf16)


def chip_kernel(mine_ref, got_ref, near_ref, far_ref):
    half = near_ref.shape[0]
    near_ref[...] = mine_ref[:half] + got_ref[:half].astype(f32)
    far_ref[...] = (mine_ref[half:] + got_ref[half:].astype(f32)).astype(bf16)


def pair_kernel(goes_ref, near_ref, got_ref, mine_ref, send_ref, pick_ref):
    mine_ref[...] = near_ref[0] + got_ref[0].astype(f32)
    send_ref[...] = (near_ref[1] + got_ref[1].astype(f32)).astype(bf16)
    rows, columns = mine_ref.shape
    chunks = columns // lanes
    goes = column_of(goes_ref[...]) * chunks
    for k in range(chunks):
        pick_ref[k * rows : (k + 1) * rows, :] = one_hot(
            iota((rows, pick_ref.shape[1]), 1) == goes + k
        )


def named_here(requested_ref, present):
    owner = lax.axis_index("replica")
    requested = requested_ref[...]
    groups = requested.shape[0]
    mine = lax.div(requested, jnp.int32(present)) == owner
    which = jnp.sum(
        jnp.where(mine, lax.rem(requested, jnp.int32(present)), 0), axis=1, keepdims=True
    )
    placed = iota((groups, groups), 1) == place_in_order(iota((groups, groups), 0), groups)
    which = jnp.sum(jnp.where(placed, which, 0), axis=0, keepdims=True)
    return column_of(which)


def interleave(parts, backward):
    shape = (parts * block, parts * block)
    row, column = iota(shape, 0), iota(shape, 1)
    if backward:
        row, column = column, row
    return one_hot(lax.rem(row, jnp.int32(parts)) * block + lax.div(row, jnp.int32(parts)) == column)


def low_kernel(which_ref, here_ref, down_ref, up_ref, out_ref, rows_ref):
    present, rank, features = down_ref.shape
    groups = which_ref.shape[0]
    chunks = features // lanes
    parts = most * chunks
    order = interleave(parts, True)
    for b in range(groups // block):
        rows = times(order, here_ref[b * parts * block : (b + 1) * parts * block, :]).astype(bf16)
        for j in range(parts):
            place, k = divmod(j, chunks)
            rows_ref[
                place * groups + b * block : place * groups + (b + 1) * block,
                k * lanes : (k + 1) * lanes,
            ] = rows[j * block : (j + 1) * block, :]
    down = jnp.concatenate([down_ref[a] for a in range(present)], axis=0)
    low = lax.dot_general(
        rows_ref[...], down, (((1,), (1,)), ((), ())), preferred_element_type=f32
    )
    which = which_ref[...]
    places = []
    for place in range(most):
        one = low[place * groups : (place + 1) * groups, :]
        places.append(
            sum(
                jnp.where(which == a, one[:, a * rank : (a + 1) * rank], 0.0)
                for a in range(present)
            )
        )
    low = jnp.concatenate(places, axis=1).astype(bf16)
    up = jnp.concatenate([up_ref[a] for a in range(present)], axis=0)
    height = up.shape[0]
    shards = out_ref.shape[0]
    columns = up.shape[1] // shards
    for peer in range(shards):
        for k in range(columns // lanes):
            out_ref[peer, k * height : (k + 1) * height, :] = up[
                :, peer * columns + k * lanes : peer * columns + (k + 1) * lanes
            ]
        out_ref[peer, out_ref.shape[1] - groups :, :] = low


def result_kernel(present, which_ref, low_ref, up_ref, out_ref, rows_ref):
    shards, groups, width = low_ref.shape
    rank = width // most
    window = rank // shards
    depth = shards * present * window
    chunks = up_ref.shape[1] // (present * window)
    parts = most * chunks
    low = low_ref[0].astype(f32)
    for peer in range(1, shards):
        low = low + low_ref[peer].astype(f32)
    low = (adapter_scale * low).astype(bf16)
    up = jnp.concatenate(
        [
            jnp.concatenate(
                [up_ref[peer, k * present * window : (k + 1) * present * window, :] for peer in range(shards)],
                axis=0,
            )
            for k in range(chunks)
        ],
        axis=1,
    )
    which = which_ref[...]
    source, target = iota((width, depth), 0), iota((width, depth), 1)
    shard = lax.div(target, jnp.int32(present * window))
    rank_of = shard * window + lax.rem(target, jnp.int32(window))
    adapter = iota((groups, depth), 1)
    adapter = lax.rem(lax.div(adapter, jnp.int32(window)), jnp.int32(present))
    order = interleave(parts, False)
    spread = times(
        low,
        jnp.concatenate([one_hot(source == place * rank + rank_of) for place in range(most)], axis=1),
    ).astype(bf16)
    spread = jnp.concatenate(
        [
            jnp.where(adapter == which, spread[:, place * depth : (place + 1) * depth], jnp.zeros((), bf16))
            for place in range(most)
        ],
        axis=0,
    )
    results = times(spread, up).astype(bf16)
    for b in range(groups // block):
        for j in range(parts):
            place, k = divmod(j, chunks)
            start = place * groups + b * block
            rows_ref[j * block : (j + 1) * block, :] = results[
                start : start + block, k * lanes : (k + 1) * lanes
            ]
        out_ref[b * parts * block : (b + 1) * parts * block, :] = times(order, rows_ref[...]).astype(bf16)


def lora_kernel(pick_ref, back_ref, out_ref):
    rows, columns = out_ref.shape
    mine = times(pick_ref[...], back_ref[...])
    for k in range(columns // lanes):
        out_ref[:, k * lanes : (k + 1) * lanes] = mine[k * rows : (k + 1) * rows, :]


def finish_kernel(lora_ref, mine_ref, got_ref, out_ref):
    out_ref[...] = (mine_ref[...] + got_ref[...].astype(f32) + lora_ref[...]).astype(bf16)


def whole(shape):
    return pl.BlockSpec(shape, lambda *_: (0,) * len(shape))


def call(kernel, out_shape, in_specs, out_specs, cost=(0, 0), limit=4, **options):
    return pl.pallas_call(
        kernel,
        grid=(1,),
        out_shape=out_shape,
        in_specs=in_specs,
        out_specs=out_specs,
        compiler_params=pltpu.CompilerParams(vmem_limit_bytes=limit << 20),
        cost_estimate=pl.CostEstimate(flops=cost[0], bytes_accessed=cost[1], transcendentals=0),
        **options,
    )


def local(attention, weight, down, up, requested, slot):
    rows, features = attention.shape
    present, rank, _ = down.shape
    window = up.shape[1]
    groups = requested.shape[0]
    shards = lax.axis_size("tensor")
    columns = weight.shape[1] // shards
    parts = most * features // lanes
    out_parts = most * columns // lanes
    chunks = columns // lanes
    shape = jax.ShapeDtypeStruct
    order = [ring_order(groups)]

    sent, goes = call(
        functools.partial(send_kernel, present),
        (shape((groups * parts, lanes), bf16), shape((1, rows), i32)),
        [whole(requested.shape), whole((1, rows)), whole(attention.shape)],
        (whole((groups * parts, lanes)), whole((1, rows))),
        cost=(1 << 34, 1 << 20),
        limit=56,
    )(requested, slot.reshape(1, rows), attention)
    here = lax.all_to_all(sent.reshape(groups, parts, lanes), "replica", 0, 0, axis_index_groups=order, tiled=True)

    chips = shards // 2
    tile = (rows, columns)
    mine, other, which = call(
        functools.partial(base_kernel, present),
        (shape((chips,) + tile, f32), shape((chips,) + tile, bf16), shape((groups, 1), i32)),
        [
            whole(requested.shape),
            pl.BlockSpec(memory_space=pl.ANY),
            pl.BlockSpec(memory_space=pl.ANY),
        ],
        (whole((chips,) + tile), whole((chips,) + tile), whole((groups, 1))),
        cost=(1 << 34, 1 << 20),
        limit=51,
        scratch_shapes=[
            pltpu.VMEM((rows, features), bf16),
            pltpu.VMEM((shards, features, columns), bf16),
            pltpu.SemaphoreType.DMA((shards + 1,)),
        ],
    )(requested, attention, weight)
    got = lax.ppermute(other, "tensor", [(i, i ^ 1) for i in range(shards)])

    up_rows = chunks * present * window
    message = call(
        low_kernel,
        shape((shards, up_rows + groups, lanes), bf16),
        [whole((groups, 1)), whole((groups * parts, lanes)), whole(down.shape), whole(up.shape)],
        whole((shards, up_rows + groups, lanes)),
        cost=(6 * groups * parts * lanes * lanes, 6 * groups * parts * lanes),
        scratch_shapes=[pltpu.VMEM((most * groups, features), bf16)],
    )(which, here.reshape(groups * parts, lanes), down, up)
    message = lax.all_to_all(message, "tensor", 0, 0, tiled=True)

    near, far = call(
        chip_kernel,
        (shape((chips // 2,) + tile, f32), shape((chips // 2,) + tile, bf16)),
        [whole((chips,) + tile), whole((chips,) + tile)],
        (whole((chips // 2,) + tile), whole((chips // 2,) + tile)),
        cost=(1 << 34, 1 << 20),
    )(mine, got)
    got = lax.ppermute(far, "tensor", [(i, i ^ 4) for i in range(shards)])

    result = call(
        functools.partial(result_kernel, present),
        shape((groups * out_parts, lanes), bf16),
        [
            whole((groups, 1)),
            pl.BlockSpec((shards, groups, lanes), lambda *_: (0, up_rows // groups, 0)),
            pl.BlockSpec((shards, up_rows, lanes), lambda *_: (0, 0, 0)),
        ],
        whole((groups * out_parts, lanes)),
        cost=(6 * groups * parts * lanes * lanes, 6 * groups * parts * lanes),
        scratch_shapes=[pltpu.VMEM((out_parts * block, lanes), bf16)],
    )(which, message, message)
    back = lax.all_to_all(result.reshape(groups, out_parts, lanes), "replica", 0, 0, axis_index_groups=order, tiled=True)

    mine, send, pick = call(
        pair_kernel,
        (shape(tile, f32), shape(tile, bf16), shape((chunks * rows, groups * out_parts), bf16)),
        [whole((1, rows)), whole((chips // 2,) + tile), whole((chips // 2,) + tile)],
        (whole(tile), whole(tile), whole((chunks * rows, groups * out_parts))),
        cost=(1 << 34, 1 << 20),
    )(goes, near, got)
    got = lax.ppermute(send, "tensor", [(i, i ^ 2) for i in range(shards)])

    lora = call(
        lora_kernel,
        shape(tile, f32),
        [whole((chunks * rows, groups * out_parts)), whole((groups * out_parts, lanes))],
        whole(tile),
        cost=(2 * chunks * rows * groups * out_parts * lanes, 4 * chunks * rows * groups * out_parts),
    )(pick, back.reshape(groups * out_parts, lanes))
    return call(
        finish_kernel,
        shape(tile, bf16),
        [whole(tile), whole(tile), whole(tile)],
        whole(tile),
    )(lora, mine, got)


def solution(mesh):
    in_specs = (
        P("replica", "tensor"),
        P("tensor", None),
        P("replica", None, "tensor"),
        P("replica", "tensor", None),
        P(),
        P("replica", None),
    )
    out_specs = P("replica", "tensor")
    return jax.shard_map(local, mesh=mesh, in_specs=in_specs, out_specs=out_specs, check_vma=False)
```

```python
import functools
import math

import jax
import jax.numpy as jnp
from jax import lax
from jax.experimental import pallas as pl
from jax.experimental.pallas import tpu as pltpu
from jax.sharding import PartitionSpec as P

adapter_scale = 2.0
most = 2
lanes = 128
block = 16
first_z, first_y = 6, 5
first_shard = 6
ahead = 8
bf16 = jnp.bfloat16
f32 = jnp.float32
i32 = jnp.int32


def iota(shape, axis):
    return lax.broadcasted_iota(i32, shape, axis)


def one_hot(hit):
    return jnp.where(hit, 1.0, 0.0).astype(bf16)


def times(a, b):
    return jnp.dot(a, b, preferred_element_type=f32)


def steps_of(side):
    return [0] + sorted(range(1, side), key=lambda step: -min(step, side - step))


def ring_order(count):
    side = math.isqrt(count)
    if side * side != count:
        return list(range(count))
    steps = steps_of(side)
    return [(first_z + z) % side * side + (first_y + y) % side for z in steps for y in steps]


def place_in_order(device, count):
    side = math.isqrt(count)
    if side * side != count:
        return device

    def place(position, first):
        step = lax.rem(position + (side - first % side), jnp.int32(side))
        return sum(jnp.where(step == one, n, 0) for n, one in enumerate(steps_of(side)))

    z = place(lax.div(device, jnp.int32(side)), first_z)
    return z * side + place(lax.rem(device, jnp.int32(side)), first_y)


def column_of(row):
    size = row.shape[1]
    square = (size, size)
    return jnp.sum(jnp.where(iota(square, 0) == iota(square, 1), row, 0), axis=1, keepdims=True)


def place_rows(present, requested_ref, slot_ref):
    group = lax.axis_index("replica")
    owners = requested_ref.shape[0]
    count = slot_ref.shape[1]
    mine = iota(requested_ref.shape, 0) == group
    entries = jnp.sum(jnp.where(mine, requested_ref[...], 0), axis=0, keepdims=True)
    named = iota((owners, count), 0) == slot_ref[...]
    before = one_hot(iota((count, count), 0) < iota((count, count), 1))
    earlier = times(one_hot(named), before)
    place = jnp.sum(jnp.where(named, earlier, 0.0), axis=0, keepdims=True)
    owner = place_in_order(lax.div(entries, jnp.int32(present)), owners).astype(f32).astype(bf16)
    owner = times(jnp.broadcast_to(owner, (block, owners)), one_hot(named))[:1]
    return (owner * float(most) + place).astype(i32)


def send_kernel(present, requested_ref, slot_ref, attention_ref, sent_ref, goes_ref):
    goes = place_rows(present, requested_ref, slot_ref)
    count, features = attention_ref.shape
    chunks = features // lanes
    goes_ref[...] = goes
    target = jnp.concatenate([goes * chunks + k for k in range(chunks)], axis=1)
    stacked = jnp.concatenate(
        [attention_ref[:, k * lanes : (k + 1) * lanes] for k in range(chunks)], axis=0
    )
    pick = one_hot(iota((sent_ref.shape[0], chunks * count), 0) == target)
    sent_ref[...] = times(pick, stacked).astype(bf16)


def base_kernel(
    present,
    requested_ref,
    attention_ref,
    weight_ref,
    mine_ref,
    other_ref,
    which_ref,
    rows,
    weights,
    arrived,
):
    chips, _, columns = mine_ref.shape
    index = lax.axis_index("tensor")
    core = lax.rem(index, 2)
    chip = lax.div(index, 2)

    def fetch(slot):
        away = slot // 2
        device = 2 * (chip ^ away) + (core if slot % 2 else 1 - core)
        start = pl.multiple_of(device * columns, columns)
        return pltpu.make_async_copy(
            weight_ref.at[:, pl.ds(start, columns)], weights.at[slot], arrived.at[slot]
        )

    load = pltpu.make_async_copy(attention_ref, rows, arrived.at[2 * chips])
    load.start()
    for slot in range(ahead):
        fetch(slot).start()
    which_ref[...] = named_here(requested_ref, present)
    load.wait()
    for slot in range(2 * chips):
        fetch(slot).wait()
        if slot + ahead < 2 * chips:
            fetch(slot + ahead).start()
        base = times(rows[...], weights[slot])
        if slot % 2:
            mine_ref[slot // 2] = base
        else:
            other_ref[slot // 2] = base.astype(bf16)


def chip_kernel(mine_ref, got_ref, near_ref, far_ref):
    half = near_ref.shape[0]
    near_ref[...] = mine_ref[:half] + got_ref[:half].astype(f32)
    far_ref[...] = (mine_ref[half:] + got_ref[half:].astype(f32)).astype(bf16)


def pair_kernel(goes_ref, near_ref, got_ref, mine_ref, send_ref, pick_ref):
    mine_ref[...] = near_ref[0] + got_ref[0].astype(f32)
    send_ref[...] = (near_ref[1] + got_ref[1].astype(f32)).astype(bf16)
    rows, columns = mine_ref.shape
    chunks = columns // lanes
    goes = column_of(goes_ref[...]) * chunks
    for k in range(chunks):
        pick_ref[k * rows : (k + 1) * rows, :] = one_hot(
            iota((rows, pick_ref.shape[1]), 1) == goes + k
        )


def named_here(requested_ref, present):
    owner = lax.axis_index("replica")
    requested = requested_ref[...]
    groups = requested.shape[0]
    mine = lax.div(requested, jnp.int32(present)) == owner
    which = jnp.sum(
        jnp.where(mine, lax.rem(requested, jnp.int32(present)), 0), axis=1, keepdims=True
    )
    placed = iota((groups, groups), 1) == place_in_order(iota((groups, groups), 0), groups)
    which = jnp.sum(jnp.where(placed, which, 0), axis=0, keepdims=True)
    return column_of(which)


def interleave(parts, backward):
    shape = (parts * block, parts * block)
    row, column = iota(shape, 0), iota(shape, 1)
    if backward:
        row, column = column, row
    return one_hot(lax.rem(row, jnp.int32(parts)) * block + lax.div(row, jnp.int32(parts)) == column)


def low_kernel(which_ref, here_ref, down_ref, up_ref, out_ref, rows_ref):
    present, rank, features = down_ref.shape
    groups = which_ref.shape[0]
    chunks = features // lanes
    parts = most * chunks
    order = interleave(parts, True)
    for b in range(groups // block):
        rows = times(order, here_ref[b * parts * block : (b + 1) * parts * block, :]).astype(bf16)
        for j in range(parts):
            place, k = divmod(j, chunks)
            rows_ref[
                place * groups + b * block : place * groups + (b + 1) * block,
                k * lanes : (k + 1) * lanes,
            ] = rows[j * block : (j + 1) * block, :]
    down = jnp.concatenate([down_ref[a] for a in range(present)], axis=0)
    low = lax.dot_general(
        rows_ref[...], down, (((1,), (1,)), ((), ())), preferred_element_type=f32
    )
    which = which_ref[...]
    places = []
    for place in range(most):
        one = low[place * groups : (place + 1) * groups, :]
        places.append(
            sum(
                jnp.where(which == a, one[:, a * rank : (a + 1) * rank], 0.0)
                for a in range(present)
            )
        )
    low = jnp.concatenate(places, axis=1).astype(bf16)
    up = jnp.concatenate([up_ref[a] for a in range(present)], axis=0)
    height = up.shape[0]
    shards = out_ref.shape[0]
    columns = up.shape[1] // shards
    for peer in range(shards):
        device = (first_shard + peer) % shards
        for k in range(columns // lanes):
            out_ref[peer, k * height : (k + 1) * height, :] = up[
                :, device * columns + k * lanes : device * columns + (k + 1) * lanes
            ]
        out_ref[peer, out_ref.shape[1] - groups :, :] = low


def result_kernel(present, which_ref, low_ref, up_ref, out_ref, rows_ref):
    shards, groups, width = low_ref.shape
    rank = width // most
    window = rank // shards
    depth = shards * present * window
    chunks = up_ref.shape[1] // (present * window)
    parts = most * chunks
    low = low_ref[0].astype(f32)
    for peer in range(1, shards):
        low = low + low_ref[peer].astype(f32)
    low = (adapter_scale * low).astype(bf16)
    up = jnp.concatenate(
        [
            jnp.concatenate(
                [up_ref[peer, k * present * window : (k + 1) * present * window, :] for peer in range(shards)],
                axis=0,
            )
            for k in range(chunks)
        ],
        axis=1,
    )
    which = which_ref[...]
    source, target = iota((width, depth), 0), iota((width, depth), 1)
    shard = lax.rem(lax.div(target, jnp.int32(present * window)) + first_shard, jnp.int32(shards))
    rank_of = shard * window + lax.rem(target, jnp.int32(window))
    adapter = iota((groups, depth), 1)
    adapter = lax.rem(lax.div(adapter, jnp.int32(window)), jnp.int32(present))
    order = interleave(parts, False)
    spread = times(
        low,
        jnp.concatenate([one_hot(source == place * rank + rank_of) for place in range(most)], axis=1),
    ).astype(bf16)
    spread = jnp.concatenate(
        [
            jnp.where(adapter == which, spread[:, place * depth : (place + 1) * depth], jnp.zeros((), bf16))
            for place in range(most)
        ],
        axis=0,
    )
    results = times(spread, up).astype(bf16)
    for b in range(groups // block):
        for j in range(parts):
            place, k = divmod(j, chunks)
            start = place * groups + b * block
            rows_ref[j * block : (j + 1) * block, :] = results[
                start : start + block, k * lanes : (k + 1) * lanes
            ]
        out_ref[b * parts * block : (b + 1) * parts * block, :] = times(order, rows_ref[...]).astype(bf16)


def lora_kernel(pick_ref, back_ref, out_ref):
    rows, columns = out_ref.shape
    mine = times(pick_ref[...], back_ref[...])
    for k in range(columns // lanes):
        out_ref[:, k * lanes : (k + 1) * lanes] = mine[k * rows : (k + 1) * rows, :]


def finish_kernel(lora_ref, mine_ref, got_ref, out_ref):
    out_ref[...] = (mine_ref[...] + got_ref[...].astype(f32) + lora_ref[...]).astype(bf16)


def whole(shape):
    return pl.BlockSpec(shape, lambda *_: (0,) * len(shape))


def call(kernel, out_shape, in_specs, out_specs, cost=(0, 0), limit=4, **options):
    return pl.pallas_call(
        kernel,
        grid=(1,),
        out_shape=out_shape,
        in_specs=in_specs,
        out_specs=out_specs,
        compiler_params=pltpu.CompilerParams(vmem_limit_bytes=limit << 20),
        cost_estimate=pl.CostEstimate(flops=cost[0], bytes_accessed=cost[1], transcendentals=0),
        **options,
    )


def local(attention, weight, down, up, requested, slot):
    rows, features = attention.shape
    present, rank, _ = down.shape
    window = up.shape[1]
    groups = requested.shape[0]
    shards = lax.axis_size("tensor")
    columns = weight.shape[1] // shards
    parts = most * features // lanes
    out_parts = most * columns // lanes
    chunks = columns // lanes
    shape = jax.ShapeDtypeStruct
    order = [ring_order(groups)]

    sent, goes = call(
        functools.partial(send_kernel, present),
        (shape((groups * parts, lanes), bf16), shape((1, rows), i32)),
        [whole(requested.shape), whole((1, rows)), whole(attention.shape)],
        (whole((groups * parts, lanes)), whole((1, rows))),
        cost=(1 << 34, 1 << 20),
        limit=56,
    )(requested, slot.reshape(1, rows), attention)
    here = lax.all_to_all(sent.reshape(groups, parts, lanes), "replica", 0, 0, axis_index_groups=order, tiled=True)

    chips = shards // 2
    tile = (rows, columns)
    mine, other, which = call(
        functools.partial(base_kernel, present),
        (shape((chips,) + tile, f32), shape((chips,) + tile, bf16), shape((groups, 1), i32)),
        [
            whole(requested.shape),
            pl.BlockSpec(memory_space=pl.ANY),
            pl.BlockSpec(memory_space=pl.ANY),
        ],
        (whole((chips,) + tile), whole((chips,) + tile), whole((groups, 1))),
        cost=(1 << 34, 1 << 20),
        limit=51,
        scratch_shapes=[
            pltpu.VMEM((rows, features), bf16),
            pltpu.VMEM((shards, features, columns), bf16),
            pltpu.SemaphoreType.DMA((shards + 1,)),
        ],
    )(requested, attention, weight)
    got = lax.ppermute(other, "tensor", [(i, i ^ 1) for i in range(shards)])

    up_rows = chunks * present * window
    message = call(
        low_kernel,
        shape((shards, up_rows + groups, lanes), bf16),
        [whole((groups, 1)), whole((groups * parts, lanes)), whole(down.shape), whole(up.shape)],
        whole((shards, up_rows + groups, lanes)),
        cost=(6 * groups * parts * lanes * lanes, 6 * groups * parts * lanes),
        scratch_shapes=[pltpu.VMEM((most * groups, features), bf16)],
    )(which, here.reshape(groups * parts, lanes), down, up)
    shard_order = [[(first_shard + n) % shards for n in range(shards)]]
    message = lax.all_to_all(
        message, "tensor", 0, 0, axis_index_groups=shard_order, tiled=True
    )

    near, far = call(
        chip_kernel,
        (shape((chips // 2,) + tile, f32), shape((chips // 2,) + tile, bf16)),
        [whole((chips,) + tile), whole((chips,) + tile)],
        (whole((chips // 2,) + tile), whole((chips // 2,) + tile)),
        cost=(1 << 34, 1 << 20),
    )(mine, got)
    got = lax.ppermute(far, "tensor", [(i, i ^ 4) for i in range(shards)])

    result = call(
        functools.partial(result_kernel, present),
        shape((groups * out_parts, lanes), bf16),
        [
            whole((groups, 1)),
            pl.BlockSpec((shards, groups, lanes), lambda *_: (0, up_rows // groups, 0)),
            pl.BlockSpec((shards, up_rows, lanes), lambda *_: (0, 0, 0)),
        ],
        whole((groups * out_parts, lanes)),
        cost=(6 * groups * parts * lanes * lanes, 6 * groups * parts * lanes),
        scratch_shapes=[pltpu.VMEM((out_parts * block, lanes), bf16)],
    )(which, message, message)
    back = lax.all_to_all(result.reshape(groups, out_parts, lanes), "replica", 0, 0, axis_index_groups=order, tiled=True)

    mine, send, pick = call(
        pair_kernel,
        (shape(tile, f32), shape(tile, bf16), shape((chunks * rows, groups * out_parts), bf16)),
        [whole((1, rows)), whole((chips // 2,) + tile), whole((chips // 2,) + tile)],
        (whole(tile), whole(tile), whole((chunks * rows, groups * out_parts))),
        cost=(1 << 34, 1 << 20),
    )(goes, near, got)
    got = lax.ppermute(send, "tensor", [(i, i ^ 2) for i in range(shards)])

    lora = call(
        lora_kernel,
        shape(tile, f32),
        [whole((chunks * rows, groups * out_parts)), whole((groups * out_parts, lanes))],
        whole(tile),
        cost=(2 * chunks * rows * groups * out_parts * lanes, 4 * chunks * rows * groups * out_parts),
    )(pick, back.reshape(groups * out_parts, lanes))
    return call(
        finish_kernel,
        shape(tile, bf16),
        [whole(tile), whole(tile), whole(tile)],
        whole(tile),
    )(lora, mine, got)


def solution(mesh):
    in_specs = (
        P("replica", "tensor"),
        P("tensor", None),
        P("replica", None, "tensor"),
        P("replica", "tensor", None),
        P(),
        P("replica", None),
    )
    out_specs = P("replica", "tensor")
    return jax.shard_map(local, mesh=mesh, in_specs=in_specs, out_specs=out_specs, check_vma=False)
```

```python
import functools
import math

import jax
import jax.numpy as jnp
from jax import lax
from jax.experimental import pallas as pl
from jax.experimental.pallas import tpu as pltpu
from jax.sharding import PartitionSpec as P

adapter_scale = 2.0
most = 2
lanes = 128
block = 16
first_z, first_y = 6, 5
first_shard = 6
bf16 = jnp.bfloat16
f32 = jnp.float32
i32 = jnp.int32


def iota(shape, axis):
    return lax.broadcasted_iota(i32, shape, axis)


def one_hot(hit):
    return jnp.where(hit, 1.0, 0.0).astype(bf16)


def times(a, b):
    return jnp.dot(a, b, preferred_element_type=f32)


def steps_of(side):
    return [0] + sorted(range(1, side), key=lambda step: -min(step, side - step))


def ring_order(count):
    side = math.isqrt(count)
    if side * side != count:
        return list(range(count))
    steps = steps_of(side)
    return [(first_z + z) % side * side + (first_y + y) % side for z in steps for y in steps]


def place_in_order(device, count):
    side = math.isqrt(count)
    if side * side != count:
        return device

    def place(position, first):
        step = lax.rem(position + (side - first % side), jnp.int32(side))
        return sum(jnp.where(step == one, n, 0) for n, one in enumerate(steps_of(side)))

    z = place(lax.div(device, jnp.int32(side)), first_z)
    return z * side + place(lax.rem(device, jnp.int32(side)), first_y)


def column_of(row):
    size = row.shape[1]
    square = (size, size)
    return jnp.sum(jnp.where(iota(square, 0) == iota(square, 1), row, 0), axis=1, keepdims=True)


def place_rows(present, requested_ref, slot_ref):
    group = lax.axis_index("replica")
    owners = requested_ref.shape[0]
    count = slot_ref.shape[1]
    mine = iota(requested_ref.shape, 0) == group
    entries = jnp.sum(jnp.where(mine, requested_ref[...], 0), axis=0, keepdims=True)
    named = iota((owners, count), 0) == slot_ref[...]
    before = one_hot(iota((count, count), 0) < iota((count, count), 1))
    earlier = times(one_hot(named), before)
    place = jnp.sum(jnp.where(named, earlier, 0.0), axis=0, keepdims=True)
    owner = place_in_order(lax.div(entries, jnp.int32(present)), owners).astype(f32).astype(bf16)
    owner = times(jnp.broadcast_to(owner, (block, owners)), one_hot(named))[:1]
    return (owner * float(most) + place).astype(i32)


def send_kernel(present, requested_ref, slot_ref, attention_ref, sent_ref, goes_ref):
    goes = place_rows(present, requested_ref, slot_ref)
    count, features = attention_ref.shape
    chunks = features // lanes
    goes_ref[...] = goes
    target = jnp.concatenate([goes * chunks + k for k in range(chunks)], axis=1)
    stacked = jnp.concatenate(
        [attention_ref[:, k * lanes : (k + 1) * lanes] for k in range(chunks)], axis=0
    )
    pick = one_hot(iota((sent_ref.shape[0], chunks * count), 0) == target)
    sent_ref[...] = times(pick, stacked).astype(bf16)


def fetches(weight_ref, weights, arrived, other_core):
    chips, _, columns = weights.shape
    index = lax.axis_index("tensor")
    core = lax.rem(index, 2)
    chip = lax.div(index, 2)
    copies = []
    for away in range(chips):
        device = 2 * (chip ^ away) + (1 - core if other_core else core)
        start = pl.multiple_of(device * columns, columns)
        copies.append(
            pltpu.make_async_copy(
                weight_ref.at[:, pl.ds(start, columns)], weights.at[away], arrived.at[away]
            )
        )
    return copies


def other_kernel(
    present, requested_ref, attention_ref, weight_ref, other_ref, which_ref, rows, weights, arrived
):
    load = pltpu.make_async_copy(attention_ref, rows, arrived.at[weights.shape[0]])
    load.start()
    copies = fetches(weight_ref, weights, arrived, True)
    for copy in copies:
        copy.start()
    which_ref[...] = named_here(requested_ref, present)
    load.wait()
    for away, copy in enumerate(copies):
        copy.wait()
        other_ref[away] = times(rows[...], weights[away]).astype(bf16)


def chip_kernel(attention_ref, weight_ref, got_ref, near_ref, far_ref, rows, weights, arrived):
    load = pltpu.make_async_copy(attention_ref, rows, arrived.at[weights.shape[0]])
    load.start()
    copies = fetches(weight_ref, weights, arrived, False)
    for copy in copies:
        copy.start()
    load.wait()
    half = near_ref.shape[0]
    for away, copy in enumerate(copies):
        copy.wait()
        total = times(rows[...], weights[away]) + got_ref[away].astype(f32)
        if away < half:
            near_ref[away] = total
        else:
            far_ref[away - half] = total.astype(bf16)


def pair_kernel(goes_ref, near_ref, got_ref, mine_ref, send_ref, pick_ref):
    mine_ref[...] = near_ref[0] + got_ref[0].astype(f32)
    send_ref[...] = (near_ref[1] + got_ref[1].astype(f32)).astype(bf16)
    rows, columns = mine_ref.shape
    chunks = columns // lanes
    goes = column_of(goes_ref[...]) * chunks
    for k in range(chunks):
        pick_ref[k * rows : (k + 1) * rows, :] = one_hot(
            iota((rows, pick_ref.shape[1]), 1) == goes + k
        )


def named_here(requested_ref, present):
    owner = lax.axis_index("replica")
    requested = requested_ref[...]
    groups = requested.shape[0]
    mine = lax.div(requested, jnp.int32(present)) == owner
    which = jnp.sum(
        jnp.where(mine, lax.rem(requested, jnp.int32(present)), 0), axis=1, keepdims=True
    )
    placed = iota((groups, groups), 1) == place_in_order(iota((groups, groups), 0), groups)
    which = jnp.sum(jnp.where(placed, which, 0), axis=0, keepdims=True)
    return column_of(which)


def interleave(parts, backward):
    shape = (parts * block, parts * block)
    row, column = iota(shape, 0), iota(shape, 1)
    if backward:
        row, column = column, row
    return one_hot(lax.rem(row, jnp.int32(parts)) * block + lax.div(row, jnp.int32(parts)) == column)


def low_kernel(which_ref, here_ref, down_ref, up_ref, out_ref, rows_ref):
    present, rank, features = down_ref.shape
    groups = which_ref.shape[0]
    chunks = features // lanes
    parts = most * chunks
    order = interleave(parts, True)
    for b in range(groups // block):
        rows = times(order, here_ref[b * parts * block : (b + 1) * parts * block, :]).astype(bf16)
        for j in range(parts):
            place, k = divmod(j, chunks)
            rows_ref[
                place * groups + b * block : place * groups + (b + 1) * block,
                k * lanes : (k + 1) * lanes,
            ] = rows[j * block : (j + 1) * block, :]
    down = jnp.concatenate([down_ref[a] for a in range(present)], axis=0)
    low = lax.dot_general(
        rows_ref[...], down, (((1,), (1,)), ((), ())), preferred_element_type=f32
    )
    which = which_ref[...]
    places = []
    for place in range(most):
        one = low[place * groups : (place + 1) * groups, :]
        places.append(
            sum(
                jnp.where(which == a, one[:, a * rank : (a + 1) * rank], 0.0)
                for a in range(present)
            )
        )
    low = jnp.concatenate(places, axis=1).astype(bf16)
    up = jnp.concatenate([up_ref[a] for a in range(present)], axis=0)
    height = up.shape[0]
    shards = out_ref.shape[0]
    columns = up.shape[1] // shards
    for peer in range(shards):
        device = (first_shard + peer) % shards
        for k in range(columns // lanes):
            out_ref[peer, k * height : (k + 1) * height, :] = up[
                :, device * columns + k * lanes : device * columns + (k + 1) * lanes
            ]
        out_ref[peer, out_ref.shape[1] - groups :, :] = low


def result_kernel(present, which_ref, low_ref, up_ref, out_ref, rows_ref):
    shards, groups, width = low_ref.shape
    rank = width // most
    window = rank // shards
    depth = shards * present * window
    chunks = up_ref.shape[1] // (present * window)
    parts = most * chunks
    low = low_ref[0].astype(f32)
    for peer in range(1, shards):
        low = low + low_ref[peer].astype(f32)
    low = (adapter_scale * low).astype(bf16)
    up = jnp.concatenate(
        [
            jnp.concatenate(
                [up_ref[peer, k * present * window : (k + 1) * present * window, :] for peer in range(shards)],
                axis=0,
            )
            for k in range(chunks)
        ],
        axis=1,
    )
    which = which_ref[...]
    source, target = iota((width, depth), 0), iota((width, depth), 1)
    shard = lax.rem(lax.div(target, jnp.int32(present * window)) + first_shard, jnp.int32(shards))
    rank_of = shard * window + lax.rem(target, jnp.int32(window))
    adapter = iota((groups, depth), 1)
    adapter = lax.rem(lax.div(adapter, jnp.int32(window)), jnp.int32(present))
    order = interleave(parts, False)
    spread = times(
        low,
        jnp.concatenate([one_hot(source == place * rank + rank_of) for place in range(most)], axis=1),
    ).astype(bf16)
    spread = jnp.concatenate(
        [
            jnp.where(adapter == which, spread[:, place * depth : (place + 1) * depth], jnp.zeros((), bf16))
            for place in range(most)
        ],
        axis=0,
    )
    results = times(spread, up).astype(bf16)
    for b in range(groups // block):
        for j in range(parts):
            place, k = divmod(j, chunks)
            start = place * groups + b * block
            rows_ref[j * block : (j + 1) * block, :] = results[
                start : start + block, k * lanes : (k + 1) * lanes
            ]
        out_ref[b * parts * block : (b + 1) * parts * block, :] = times(order, rows_ref[...]).astype(bf16)


def lora_kernel(pick_ref, back_ref, out_ref):
    rows, columns = out_ref.shape
    mine = times(pick_ref[...], back_ref[...])
    for k in range(columns // lanes):
        out_ref[:, k * lanes : (k + 1) * lanes] = mine[k * rows : (k + 1) * rows, :]


def finish_kernel(lora_ref, mine_ref, got_ref, out_ref):
    out_ref[...] = (mine_ref[...] + got_ref[...].astype(f32) + lora_ref[...]).astype(bf16)


def whole(shape):
    return pl.BlockSpec(shape, lambda *_: (0,) * len(shape))


def call(kernel, out_shape, in_specs, out_specs, cost=(0, 0), limit=4, **options):
    return pl.pallas_call(
        kernel,
        grid=(1,),
        out_shape=out_shape,
        in_specs=in_specs,
        out_specs=out_specs,
        compiler_params=pltpu.CompilerParams(vmem_limit_bytes=limit << 20),
        cost_estimate=pl.CostEstimate(flops=cost[0], bytes_accessed=cost[1], transcendentals=0),
        **options,
    )


def local(attention, weight, down, up, requested, slot):
    rows, features = attention.shape
    present, rank, _ = down.shape
    window = up.shape[1]
    groups = requested.shape[0]
    shards = lax.axis_size("tensor")
    columns = weight.shape[1] // shards
    parts = most * features // lanes
    out_parts = most * columns // lanes
    chunks = columns // lanes
    shape = jax.ShapeDtypeStruct
    order = [ring_order(groups)]

    sent, goes = call(
        functools.partial(send_kernel, present),
        (shape((groups * parts, lanes), bf16), shape((1, rows), i32)),
        [whole(requested.shape), whole((1, rows)), whole(attention.shape)],
        (whole((groups * parts, lanes)), whole((1, rows))),
        cost=(1 << 34, 1 << 20),
        limit=56,
    )(requested, slot.reshape(1, rows), attention)
    here = lax.all_to_all(sent.reshape(groups, parts, lanes), "replica", 0, 0, axis_index_groups=order, tiled=True)

    chips = shards // 2
    tile = (rows, columns)
    anywhere = pl.BlockSpec(memory_space=pl.ANY)
    streams = dict(
        cost=(1 << 34, 1 << 20),
        limit=51,
        scratch_shapes=[
            pltpu.VMEM((rows, features), bf16),
            pltpu.VMEM((chips, features, columns), bf16),
            pltpu.SemaphoreType.DMA((chips + 1,)),
        ],
    )
    other, which = call(
        functools.partial(other_kernel, present),
        (shape((chips,) + tile, bf16), shape((groups, 1), i32)),
        [whole(requested.shape), anywhere, anywhere],
        (whole((chips,) + tile), whole((groups, 1))),
        **streams,
    )(requested, attention, weight)
    got = lax.ppermute(other, "tensor", [(i, i ^ 1) for i in range(shards)])

    up_rows = chunks * present * window
    message = call(
        low_kernel,
        shape((shards, up_rows + groups, lanes), bf16),
        [whole((groups, 1)), whole((groups * parts, lanes)), whole(down.shape), whole(up.shape)],
        whole((shards, up_rows + groups, lanes)),
        cost=(6 * groups * parts * lanes * lanes, 6 * groups * parts * lanes),
        scratch_shapes=[pltpu.VMEM((most * groups, features), bf16)],
    )(which, here.reshape(groups * parts, lanes), down, up)
    shard_order = [[(first_shard + n) % shards for n in range(shards)]]
    message = lax.all_to_all(
        message, "tensor", 0, 0, axis_index_groups=shard_order, tiled=True
    )

    near, far = call(
        chip_kernel,
        (shape((chips // 2,) + tile, f32), shape((chips // 2,) + tile, bf16)),
        [anywhere, anywhere, whole((chips,) + tile)],
        (whole((chips // 2,) + tile), whole((chips // 2,) + tile)),
        **streams,
    )(attention, weight, got)
    got = lax.ppermute(far, "tensor", [(i, i ^ 4) for i in range(shards)])

    result = call(
        functools.partial(result_kernel, present),
        shape((groups * out_parts, lanes), bf16),
        [
            whole((groups, 1)),
            pl.BlockSpec((shards, groups, lanes), lambda *_: (0, up_rows // groups, 0)),
            pl.BlockSpec((shards, up_rows, lanes), lambda *_: (0, 0, 0)),
        ],
        whole((groups * out_parts, lanes)),
        cost=(6 * groups * parts * lanes * lanes, 6 * groups * parts * lanes),
        scratch_shapes=[pltpu.VMEM((out_parts * block, lanes), bf16)],
    )(which, message, message)
    back = lax.all_to_all(result.reshape(groups, out_parts, lanes), "replica", 0, 0, axis_index_groups=order, tiled=True)

    mine, send, pick = call(
        pair_kernel,
        (shape(tile, f32), shape(tile, bf16), shape((chunks * rows, groups * out_parts), bf16)),
        [whole((1, rows)), whole((chips // 2,) + tile), whole((chips // 2,) + tile)],
        (whole(tile), whole(tile), whole((chunks * rows, groups * out_parts))),
        cost=(1 << 34, 1 << 20),
    )(goes, near, got)
    got = lax.ppermute(send, "tensor", [(i, i ^ 2) for i in range(shards)])

    lora = call(
        lora_kernel,
        shape(tile, f32),
        [whole((chunks * rows, groups * out_parts)), whole((groups * out_parts, lanes))],
        whole(tile),
        cost=(2 * chunks * rows * groups * out_parts * lanes, 4 * chunks * rows * groups * out_parts),
    )(pick, back.reshape(groups * out_parts, lanes))
    return call(
        finish_kernel,
        shape(tile, bf16),
        [whole(tile), whole(tile), whole(tile)],
        whole(tile),
    )(lora, mine, got)


def solution(mesh):
    in_specs = (
        P("replica", "tensor"),
        P("tensor", None),
        P("replica", None, "tensor"),
        P("replica", "tensor", None),
        P(),
        P("replica", None),
    )
    out_specs = P("replica", "tensor")
    return jax.shard_map(local, mesh=mesh, in_specs=in_specs, out_specs=out_specs, check_vma=False)
```
